32 devices in a mesh: ev: 8 (over y, x, core), ch: 4 (over z).
Axes of the slice: x: 2, y: 2, z: 4, core: 2. Of those that a mesh axis runs over, the one named last changes fastest.
Arguments:
- spectra: float32 [128, 16, 16384], P('ev', None, 'ch'), as said below
- tile_mask: int32 [128, 128], P('ev', 'ch'), may hold values 0 or 1
- source_init: float32 [128, 16], P('ev'), may hold values from -6 to 6
- site_init: float32 [16, 16384], P(None, 'ch'), may hold values from -6 to 6
- event_pos: float32 [3, 128], P(None, 'ev'), may hold values from 5 to 50
- channel_pos: float32 [2, 16384], P(None, 'ch'), may hold values from 0 to 50
- atten: float32 [16], replicated, may hold values from 0.02 to 0.3
Outputs:
- source: float32 [128, 16], P('ev')
- site: float32 [16, 16384], P(None, 'ch')
The draws below stay inside these ranges and needn't reach their ends.
Inputs may be any that keep to these rules, and one draw needn't show every extreme that they name: spectra are log amplitudes of order one to a few, with outliers. `tile_mask`: 0 marks an event invalid on a whole tile of 128 channels.
All inputs are finite; a program needn't handle non-finite values. No bound on the sum of `tile_mask` on one device may be relied on, other than what follows from the above.
Results may differ from the reference program's by a relative error of at most 0.0001.
Values sent between devices are 32-bit elements; how exact they have to be, the bound alone decides.
No kernel may reach another device: no remote copies, remote signals or barrier semaphores. Data moves between devices by JAX's collectives and lax.ppermute only.
A program may use at most 64 MiB of HBM per device.

```python
import math
import jax
import jax.numpy as jnp
from jax import lax

EV_DEV = 16
FREQS = 16
ITERS = 2
EVENTS = 128
CHANNELS = 16384


def draw_spectra(key, part):
    keys = jax.random.split(key, 7)
    src_true = 2.0 * jax.random.normal(keys[0], (EVENTS, FREQS, 1), jnp.float32)
    site_true = jax.random.normal(keys[1], (1, FREQS, CHANNELS), jnp.float32)
    ev_scale = jnp.exp(jax.random.uniform(keys[2], (EVENTS, 1, 1), jnp.float32) * 2.302585)
    ch_scale = jnp.exp(jax.random.uniform(keys[3], (1, 1, CHANNELS), jnp.float32) * 2.302585)
    outlier = jax.random.bernoulli(keys[5], 0.05, (EVENTS, FREQS, CHANNELS)).astype(jnp.float32)
    sign = jnp.where(jax.random.bernoulli(keys[6], 0.5, (EVENTS, FREQS, CHANNELS)), 1.0, -1.0)
    noise = jax.random.normal(keys[4], (EVENTS, FREQS, CHANNELS), jnp.float32)
    noise = jnp.clip(noise, -4.0, 4.0)
    return src_true + site_true + 0.05 * ev_scale * ch_scale * noise + 6.0 * outlier * sign


def with_ends(result, key, low, high):
    longest = result.shape.index(max(result.shape))
    spots = []
    for shift in (0, 1):
        where = [jax.random.randint(jax.random.fold_in(key, axis), (), 0, length) for axis, length in enumerate(result.shape)]
        where[longest] = (where[longest] + shift) % result.shape[longest]
        spots.append(tuple(where))
    return result.at[spots[0]].set(low).at[spots[1]].set(high)


def level_of(rng, dims, cuts, least, largest):
    level, own = 1.0, jax.random.fold_in(rng, 6)
    for dim, shards_of in cuts:
        draws = jnp.exp(jax.random.uniform(jax.random.fold_in(own, dim), (shards_of,), jnp.float32, least / len(cuts), largest / len(cuts)))
        level = level * jnp.repeat(draws, dims[dim] // shards_of).reshape([-1 if axis == dim else 1 for axis in range(len(dims))])
    return level


def normal_values(own_key, shape, deviation, most, pieces=(), held_as=jnp.bfloat16):
    result = jax.random.normal(own_key, shape, jnp.float32) * deviation
    if len(pieces) > 0:
        result = level_of(own_key, shape, pieces, -0.22, 0.18) * result
    return jnp.clip(result, min=-most, max=most).astype(held_as)


def setup_inputs(seed: int = 0) -> dict:
    seeds = jax.random.split(jax.random.key(seed), 8)
    spectra = draw_spectra(jax.random.fold_in(seeds[7], 71), 0)
    tile_mask = with_ends((jax.random.randint(seeds[1], (EVENTS, CHANNELS // 128), 0, 8) < 7).astype(jnp.int32), jax.random.fold_in(seeds[1], 1), 0, 1)
    source_init = normal_values(seeds[2], (EVENTS, FREQS), 1.0, 6.0, ((0, 8),), jnp.float32)
    site_init = normal_values(seeds[3], (FREQS, CHANNELS), 1.0, 6.0, ((1, 4),), jnp.float32)
    event_pos = jnp.clip(5.0 + 45.0 * jax.random.uniform(seeds[4], (3, EVENTS), jnp.float32) ** level_of(seeds[4], (3, EVENTS), ((1, 8),), -0.2, 0.2), 5.0, 50.0)
    channel_pos = jnp.clip(50.0 * jax.random.uniform(seeds[5], (2, CHANNELS), jnp.float32) ** level_of(seeds[5], (2, CHANNELS), ((1, 4),), -0.2, 0.2), 0.0, 50.0)
    atten = jnp.clip(jnp.exp(jax.random.uniform(seeds[6], (FREQS,), jnp.float32, math.log(0.02), math.log(0.3))), 0.02, 0.3)
    return dict(spectra=spectra, tile_mask=tile_mask, source_init=source_init, site_init=site_init, event_pos=event_pos, channel_pos=channel_pos, atten=atten)


def residual_block(spec, mask, src, site, pos, channel_pos, atten):
    east = pos[0][:, None] - channel_pos[0][None, :]
    north = pos[1][:, None] - channel_pos[1][None, :]
    depth = pos[2][:, None]
    travel = jnp.sqrt(east * east + north * north + depth * depth) / 3.0
    resid = spec - src[:, :, None] - site[None, :, :] + atten[None, :, None] * travel[:, None, :]
    valid = jnp.repeat(mask, 128, axis=1).astype(jnp.float32)[:, None, :]
    return (resid, valid)

def reference(spectra, tile_mask, source_init, site_init, event_pos, channel_pos, atten):
    blocks = EVENTS // EV_DEV
    spec_b = spectra.reshape(blocks, EV_DEV, FREQS, CHANNELS)
    mask_b = tile_mask.reshape(blocks, EV_DEV, CHANNELS // 128)
    pos_b = event_pos.reshape(3, blocks, EV_DEV).transpose(1, 0, 2)
    source = source_init
    site = site_init
    for step in range(ITERS):
        src_b = source.reshape(blocks, EV_DEV, FREQS)

        def stat_step(carry, xs):
            spec, mask, srcb, pos = xs
            resid, valid = residual_block(spec, mask, srcb, site, pos, channel_pos, atten)
            return ((carry[0] + lax.optimization_barrier(jnp.sum(valid * jnp.abs(resid), axis=(0, 2))), carry[1] + jnp.sum(valid)), None)
        init = (jnp.zeros((FREQS,), jnp.float32), jnp.zeros((), jnp.float32))
        (absum, count), _ = lax.scan(stat_step, init, (spec_b, mask_b, src_b, pos_b))
        delta = 1.345 * (1.2533 * absum / jnp.maximum(count, 1.0) + 1e-05)

        def weight_step(carry, xs):
            spec, mask, srcb, pos = xs
            resid, valid = residual_block(spec, mask, srcb, site, pos, channel_pos, atten)
            limit = delta[None, :, None]
            weight = limit / jnp.maximum(jnp.abs(resid), limit) * valid
            product = weight * resid
            return ((carry[0] + lax.optimization_barrier(jnp.sum(product, axis=0)), carry[1] + lax.optimization_barrier(jnp.sum(weight, axis=0))), (lax.optimization_barrier(jnp.sum(product, axis=2)), lax.optimization_barrier(jnp.sum(weight, axis=2))))
        zeros_site = jnp.zeros((FREQS, CHANNELS), jnp.float32)
        (site_num, site_den), (src_num, src_den) = lax.scan(weight_step, (zeros_site, zeros_site), (spec_b, mask_b, src_b, pos_b))
        source = source + 0.5 * src_num.reshape(EVENTS, FREQS) / (src_den.reshape(EVENTS, FREQS) + 1.0)
        site = site + 0.5 * site_num / (site_den + 1.0)
        shift = lax.optimization_barrier(jnp.sum(site, axis=1)) / CHANNELS
        site = site - shift[:, None]
        source = source + shift[None, :]
    return (source, site)
```

```python
import jax
import jax.numpy as jnp
from jax import lax
from jax.sharding import PartitionSpec as P

ITERS = 2
LANES = 128


def sum_all(vector, devices):
    sent = jnp.broadcast_to(vector, (devices, LANES))
    return jnp.sum(lax.all_to_all(sent, ("ev", "ch"), 0, 0), axis=0)


def sum_ch(value, ch_dev):
    bit = 1
    while bit < ch_dev:
        value = value + lax.ppermute(value, "ch", [(i, i ^ bit) for i in range(ch_dev)])
        bit *= 2
    return value


def on_device(spectra, tile_mask, source_init, site_init, event_pos, channel_pos, atten):
    ev_n, freqs, ch_n = spectra.shape
    ev_dev, ch_dev = lax.axis_size("ev"), lax.axis_size("ch")
    devices = ev_dev * ch_dev
    total_ch = ch_n * ch_dev
    piece = ch_n // ev_dev
    me = lax.axis_index("ev")
    valid = jnp.repeat(tile_mask, 128, axis=1).astype(jnp.float32)[:, None, :]
    count_part = jnp.sum(tile_mask.astype(jnp.float32)) * 128.0
    east = event_pos[0][:, None] - channel_pos[0][None, :]
    north = event_pos[1][:, None] - channel_pos[1][None, :]
    depth = event_pos[2][:, None]
    travel = jnp.sqrt(east * east + north * north + depth * depth) / 3.0
    path = atten[None, :, None] * travel[:, None, :]
    source = source_init
    site = site_init
    own = lax.dynamic_slice(site_init, (0, me * piece), (freqs, piece))
    count = None
    for step in range(ITERS):
        resid = spectra - source[:, :, None] - site[None, :, :] + path
        abs_part = jnp.sum(valid * jnp.abs(resid), axis=(0, 2))
        packed = jnp.concatenate([abs_part, count_part[None], jnp.zeros((LANES - freqs - 1,), jnp.float32)])
        total = sum_all(packed, devices)
        absum, count = total[:freqs], total[freqs]
        delta = 1.345 * (1.2533 * absum / jnp.maximum(count, 1.0) + 1e-05)
        limit = delta[None, :, None]
        weight = limit / jnp.maximum(jnp.abs(resid), limit) * valid
        product = weight * resid
        src = sum_ch(jnp.stack([jnp.sum(product, axis=2), jnp.sum(weight, axis=2)]), ch_dev)
        both = jnp.stack([jnp.sum(product, axis=0), jnp.sum(weight, axis=0)])
        both = both.reshape(2, freqs, ev_dev, piece).transpose(2, 0, 1, 3)
        both = jnp.sum(lax.all_to_all(both, "ev", 0, 0), axis=0)
        own = own + 0.5 * both[0] / (both[1] + 1.0)
        source = source + 0.5 * src[0] / (src[1] + 1.0)
        if step == ITERS - 1:
            sums = jnp.concatenate([jnp.sum(own, axis=1), jnp.zeros((LANES - freqs,), jnp.float32)])
            shift = sum_all(sums, devices)[:freqs] / total_ch
        sent = jnp.broadcast_to(own[None], (ev_dev, freqs, piece))
        site = lax.all_to_all(sent, "ev", 0, 0).transpose(1, 0, 2).reshape(freqs, ch_n)
    return (source + shift[None, :], site - shift[:, None])


def solution(mesh):
    in_specs = (
        P("ev", None, "ch"),
        P("ev", "ch"),
        P("ev", None),
        P(None, "ch"),
        P(None, "ev"),
        P(None, "ch"),
        P(),
    )
    out_specs = (P("ev", None), P(None, "ch"))
    return jax.shard_map(
        on_device, mesh=mesh, in_specs=in_specs, out_specs=out_specs, check_vma=False
    )
```

```python
import functools

import jax
import jax.numpy as jnp
from jax import lax
from jax.experimental import pallas as pl
from jax.experimental.pallas import tpu as pltpu
from jax.sharding import PartitionSpec as P

ITERS = 2
LANES = 128
TILE = 128
GROUP = 4
F32 = jnp.float32
VMEM = pl.BlockSpec(memory_space=pltpu.VMEM)
ANY = pl.BlockSpec(memory_space=pl.ANY)
LIMIT = 24 * 1024 * 1024


def eye(rows):
    shape = (rows, LANES)
    return lax.broadcasted_iota(jnp.int32, shape, 0) == lax.broadcasted_iota(jnp.int32, shape, 1)


def as_column(row, rows):
    spread = jnp.where(eye(rows), jnp.broadcast_to(row, (rows, LANES)), 0.0)
    return jnp.sum(spread, axis=1, keepdims=True)


def as_row(column):
    rows = column.shape[0]
    spread = jnp.where(eye(rows), jnp.broadcast_to(column, (rows, LANES)), 0.0)
    return jnp.sum(spread, axis=0, keepdims=True)


def widen(row):
    return jnp.concatenate([row, jnp.zeros((1, LANES - row.shape[1]), F32)], axis=1)


def tile_at(index):
    return pl.ds(pl.multiple_of(index * TILE, TILE), TILE)


def core_index():
    return lax.rem(lax.axis_index("ev"), 2)


def resid_kernel(spec_hbm, mask_ref, src_ref, site_ref, pos_ref, chan_ref, atten_ref,
                 mine_ref, theirs_ref, send_ref, spec, travel, source, sems):
    ev_n, freqs, ch_n = spec_hbm.shape
    half = ch_n // 2
    half_tiles = half // TILE
    core = core_index()
    copies = []
    for e in range(ev_n):
        copy = pltpu.make_async_copy(spec_hbm.at[e], spec.at[e], sems.at[e])
        copy.start()
        copies.append(copy)
    maskf = mask_ref[...].astype(F32)
    low, high = maskf[:, :half_tiles], maskf[:, half_tiles:]
    upper = core == 1
    for ref, own in ((mine_ref, True), (theirs_ref, False)):
        first, second = (high, low) if own else (low, high)
        picked = jnp.where(upper, first, second)
        for t in range(half_tiles):
            ref[ev_n, :, t * TILE:(t + 1) * TILE] = jnp.broadcast_to(picked[:, t:t + 1], (ev_n, TILE))
    count = jnp.sum(jnp.sum(maskf, axis=1, keepdims=True), axis=0, keepdims=True) * float(TILE)
    cols = [jnp.broadcast_to(as_column(widen(pos_ref[k:k + 1, :]), ev_n), (ev_n, TILE)) for k in range(3)]

    def travel_step(t, _):
        at = tile_at(t)
        east = cols[0] - chan_ref[0:1, at]
        north = cols[1] - chan_ref[1:2, at]
        travel[:, at] = jnp.sqrt(east * east + north * north + cols[2] * cols[2]) / 3.0
        return 0
    lax.fori_loop(0, ch_n // TILE, travel_step, 0, unroll=4)
    att = jnp.broadcast_to(as_column(widen(atten_ref[...]), freqs), (freqs, TILE))
    for e in range(ev_n):
        source[e] = jnp.broadcast_to(as_column(widen(src_ref[e:e + 1, :]), freqs), (freqs, TILE))
    total = jnp.zeros((freqs, TILE), F32)
    for e in range(ev_n):
        copies[e].wait()
        src = source[e]
        for ref, own in ((mine_ref, True), (theirs_ref, False)):
            base = (core if own else 1 - core) * half_tiles

            def step(t, acc, ref=ref, base=base, e=e, src=src):
                here, at = tile_at(t), tile_at(base + t)
                time = jnp.broadcast_to(travel[e:e + 1, at], (freqs, TILE))
                resid = (spec[e, :, at] - src) + (att * time - site_ref[:, at])
                ref[e, :, here] = resid
                valid = jnp.broadcast_to(ref[ev_n, e:e + 1, here], (freqs, TILE))
                return acc + jnp.abs(resid) * valid
            total = lax.fori_loop(0, half_tiles, step, total, unroll=8)
    row = as_row(jnp.sum(total, axis=1, keepdims=True))
    lane = lax.broadcasted_iota(jnp.int32, row.shape, 1)
    row = row + jnp.where(lane == freqs, jnp.broadcast_to(count, row.shape), 0.0)
    send_ref[...] = jnp.broadcast_to(row, send_ref.shape)


def weight_kernel(freqs, total_ref, count_ref, mine_ref, theirs_ref, a_ref, b_ref, src_ref):
    ev_n = mine_ref.shape[0] - 1
    half = mine_ref.shape[2]
    quarter = half // 2
    core = core_index()
    row = jnp.sum(total_ref[...], axis=0, keepdims=True)
    counts = jnp.sum(count_ref[...], axis=0, keepdims=True)
    lane = lax.broadcasted_iota(jnp.int32, row.shape, 1)
    count = jnp.sum(jnp.where(lane == freqs, counts, 0.0), axis=1, keepdims=True)
    delta = 1.345 * (1.2533 * row / jnp.maximum(count, 1.0) + 1e-05)
    delta = jnp.broadcast_to(as_column(delta, freqs), (freqs, TILE))
    per_row = LANES // freqs
    zero = jnp.zeros((freqs, TILE), F32)
    a_ref[...] = jnp.zeros_like(a_ref)
    b_ref[...] = jnp.zeros_like(b_ref)
    for which, ref in enumerate((mine_ref, theirs_ref)):
        owner = core if which == 0 else 1 - core
        nums, dens = [], []
        for start in range(0, ev_n, GROUP):
            events = range(start, start + GROUP)

            def step(t, acc, ref=ref, events=events):
                acc = list(acc)
                for out, base in ((a_ref, 0), (b_ref, quarter // TILE)):
                    here, at = tile_at(t), tile_at(base + t)
                    num, den = out[0, :, here], out[1, :, here]
                    for k, e in enumerate(events):
                        resid = ref[e, :, at]
                        valid = jnp.broadcast_to(ref[ev_n, e:e + 1, at], (freqs, TILE))
                        weight = valid * delta / jnp.maximum(jnp.abs(resid), delta)
                        product = weight * resid
                        num, den = num + product, den + weight
                        acc[2 * k] += product
                        acc[2 * k + 1] += weight
                    out[0, :, here] = num
                    out[1, :, here] = den
                return tuple(acc)
            acc = lax.fori_loop(0, quarter // TILE, step, (zero,) * (2 * GROUP))
            nums += acc[0::2]
            dens += acc[1::2]
        rows_each = ev_n // per_row
        for kind, parts in ((0, nums), (1, dens)):
            for i in range(rows_each):
                block = jnp.concatenate(parts[i * per_row:(i + 1) * per_row], axis=0)
                line = jnp.sum(block.T, axis=0, keepdims=True)
                src_ref[pl.ds(kind * 2 * rows_each + owner * rows_each + i, 1), :] = line


def increments(src_a, src_b):
    sums = src_a + src_b
    rows = sums.shape[0] // 2
    return 0.5 * sums[:rows] / (sums[rows:] + 1.0)


def site_increment(refs, at):
    num = refs[0][0, :, at] + refs[1][0, :, at]
    den = refs[0][1, :, at] + refs[1][1, :, at]
    return 0.5 * num / (den + 1.0)


def update_kernel(a0, a1, b0, b1, s0, s1, mine_ref, theirs_ref,
                  new_mine, new_theirs, dsite_ref, dsrc_ref, send_ref, shift):
    ev_n = mine_ref.shape[0] - 1
    freqs, half = mine_ref.shape[1:]
    quarter = half // 2
    core = core_index()
    dsrc = increments(s0[...], s1[...])
    dsrc_ref[...] = dsrc
    for i in range(dsrc.shape[0]):
        shift[i * LANES:(i + 1) * LANES, :] = jnp.broadcast_to(dsrc[i:i + 1, :], (LANES, LANES)).T
    for refs, base in (((a0, a1), 0), ((b0, b1), quarter // TILE)):
        for t in range(quarter // TILE):
            at = slice(t * TILE, (t + 1) * TILE)
            there = slice((base + t) * TILE, (base + t + 1) * TILE)
            dsite_ref[:, there] = site_increment(refs, at)
    total = jnp.zeros((freqs, TILE), F32)
    for which, (ref, out) in enumerate(((mine_ref, new_mine), (theirs_ref, new_theirs))):
        owner = core if which == 0 else 1 - core
        out[ev_n] = ref[ev_n]
        for e in range(ev_n):
            first = pl.multiple_of((owner * ev_n + e) * freqs, freqs)
            src = shift[pl.ds(first, freqs), :]

            def step(t, acc, ref=ref, out=out, e=e, src=src):
                at = tile_at(t)
                resid = ref[e, :, at] - src - dsite_ref[:, at]
                out[e, :, at] = resid
                valid = jnp.broadcast_to(ref[ev_n, e:e + 1, at], (freqs, TILE))
                return acc + jnp.abs(resid) * valid
            total = lax.fori_loop(0, half // TILE, step, total, unroll=8)
    row = as_row(jnp.sum(total, axis=1, keepdims=True))
    send_ref[...] = jnp.broadcast_to(row, send_ref.shape)


def site_kernel(a0, a1, b0, b1, s0, s1, site_ref, dsite_ref, dsrc_ref,
                new_ref, src_ref, send_ref):
    freqs, half = dsite_ref.shape
    quarter = half // 2
    core = core_index()
    src_ref[...] = dsrc_ref[...] + increments(s0[...], s1[...])
    total = jnp.zeros((freqs, TILE), F32)
    for refs, base in (((a0, a1), 0), ((b0, b1), quarter // TILE)):
        for t in range(quarter // TILE):
            at = slice(t * TILE, (t + 1) * TILE)
            there = slice((base + t) * TILE, (base + t + 1) * TILE)
            init = site_ref[:, tile_at(core * (half // TILE) + base + t)]
            value = init + dsite_ref[:, there] + site_increment(refs, at)
            new_ref[:, there] = value
            total = total + value
    row = as_row(jnp.sum(total, axis=1, keepdims=True))
    send_ref[...] = jnp.broadcast_to(row, send_ref.shape)


def finish_kernel(total_ch, sums_ref, mine_ref, theirs_ref, source_ref, out_source, out_site):
    freqs, half = mine_ref.shape
    core = core_index()
    row = jnp.sum(sums_ref[...], axis=0, keepdims=True) / total_ch
    column = jnp.broadcast_to(as_column(row, freqs), (freqs, TILE))
    out_source[...] = source_ref[...] + row[:, :freqs]
    for ref, owner in ((mine_ref, core), (theirs_ref, 1 - core)):
        for t in range(half // TILE):
            at = tile_at(owner * (half // TILE) + t)
            out_site[:, at] = ref[:, t * TILE:(t + 1) * TILE] - column


def call(kernel, out_shape, in_specs, scratch=()):
    outs = [jax.ShapeDtypeStruct(shape, F32) for shape in out_shape]
    return pl.pallas_call(
        kernel,
        out_shape=outs,
        in_specs=in_specs,
        out_specs=[VMEM] * len(outs),
        scratch_shapes=list(scratch),
        compiler_params=pltpu.CompilerParams(vmem_limit_bytes=LIMIT),
    )


def swap(value, axis, size, bit):
    return lax.ppermute(value, axis, [(i, i ^ bit) for i in range(size)])


def on_device(spectra, tile_mask, source_init, site_init, event_pos, channel_pos, atten):
    ev_n, freqs, ch_n = spectra.shape
    ev_dev, ch_dev = lax.axis_size("ev"), lax.axis_size("ch")
    devices = ev_dev * ch_dev
    half, quarter = ch_n // 2, ch_n // 4
    slabs = (ev_n + 1, freqs, half)
    src_rows = 2 * ev_n * freqs // LANES
    ev_bits = [1 << k for k in range(1, ev_dev.bit_length() - 1)]
    ch_bits = [1 << k for k in range(ch_dev.bit_length() - 1)]
    pairs = [[(2 * g + c) * ch_dev + z for c in range(2) for z in range(ch_dev)] for g in range(ev_dev // 2)]

    mine, theirs, sums = call(
        resid_kernel, [slabs, slabs, (devices, LANES)], [ANY] + [VMEM] * 6,
        [pltpu.VMEM(spectra.shape, F32), pltpu.VMEM((ev_n, ch_n), F32),
         pltpu.VMEM((ev_n, freqs, TILE), F32), pltpu.SemaphoreType.DMA((ev_n,))],
    )(spectra, tile_mask, source_init, site_init, event_pos, channel_pos, atten.reshape(1, freqs))
    theirs = swap(theirs, "ev", ev_dev, 1)
    first = None
    for step in range(ITERS):
        total = lax.all_to_all(sums, ("ev", "ch"), 0, 0)
        first = total if first is None else first
        a, b, src = call(
            functools.partial(weight_kernel, freqs),
            [(2, freqs, quarter), (2, freqs, quarter), (2 * src_rows, LANES)], [VMEM] * 4,
        )(total, first, mine, theirs)
        src = src + swap(src, "ev", ev_dev, 1)
        for k in range(len(ev_bits)):
            a_other = swap(a, "ev", ev_dev, ev_bits[k])
            b_other = swap(b, "ev", ev_dev, ev_bits[(k + len(ev_bits) // 2) % len(ev_bits)])
            if k < len(ev_bits) - 1:
                a, b = a + a_other, b + b_other
        for k, bit in enumerate(ch_bits):
            src_other = swap(src, "ch", ch_dev, bit)
            if k < len(ch_bits) - 1:
                src = src + src_other
        parts = (a, a_other, b, b_other, src, src_other)
        if step < ITERS - 1:
            mine, theirs, dsite, dsrc, sums = call(
                update_kernel, [slabs, slabs, (freqs, half), (src_rows, LANES), (devices, LANES)], [VMEM] * 8,
                [pltpu.VMEM((src_rows * LANES, LANES), F32)],
            )(*parts, mine, theirs)
    site, dsrc, sums = call(
        site_kernel, [(freqs, half), (src_rows, LANES), (2 * ch_dev, LANES)], [VMEM] * 9,
    )(*parts, site_init, dsite, dsrc)
    site_other = swap(site, "ev", ev_dev, 1)
    sums = lax.all_to_all(sums, ("ev", "ch"), 0, 0, axis_index_groups=pairs)
    core = lax.rem(lax.axis_index("ev"), 2)
    own = lax.dynamic_slice(dsrc, (core * (src_rows // 2), 0), (src_rows // 2, LANES))
    source = source_init + own.reshape(ev_n, freqs)
    return tuple(call(
        functools.partial(finish_kernel, float(ch_n * ch_dev)), [(ev_n, freqs), (freqs, ch_n)], [VMEM] * 4,
    )(sums, site, site_other, source))


def solution(mesh):
    in_specs = (
        P("ev", None, "ch"),
        P("ev", "ch"),
        P("ev", None),
        P(None, "ch"),
        P(None, "ev"),
        P(None, "ch"),
        P(),
    )
    out_specs = (P("ev", None), P(None, "ch"))
    return jax.shard_map(
        on_device, mesh=mesh, in_specs=in_specs, out_specs=out_specs, check_vma=False
    )
```

```python
import functools

import jax
import jax.numpy as jnp
from jax import lax
from jax.experimental import pallas as pl
from jax.experimental.pallas import tpu as pltpu
from jax.sharding import PartitionSpec as P

ITERS = 2
LANES = 128
TILE = 128
GROUP = 4
F32 = jnp.float32
VMEM = pl.BlockSpec(memory_space=pltpu.VMEM)
HBM = pl.BlockSpec(memory_space=pltpu.HBM)
LIMIT = 24 * 1024 * 1024


def eye(rows):
    shape = (rows, LANES)
    return lax.broadcasted_iota(jnp.int32, shape, 0) == lax.broadcasted_iota(jnp.int32, shape, 1)


def as_column(row, rows):
    spread = jnp.where(eye(rows), jnp.broadcast_to(row, (rows, LANES)), 0.0)
    return jnp.sum(spread, axis=1, keepdims=True)


def as_row(column):
    rows = column.shape[0]
    spread = jnp.where(eye(rows), jnp.broadcast_to(column, (rows, LANES)), 0.0)
    return jnp.sum(spread, axis=0, keepdims=True)


def widen(row):
    return jnp.concatenate([row, jnp.zeros((1, LANES - row.shape[1]), F32)], axis=1)


def tile_at(index):
    return pl.ds(pl.multiple_of(index * TILE, TILE), TILE)


def core_index():
    return lax.rem(lax.axis_index("ev"), 2)


def resid_kernel(spec_hbm, mask_hbm, src_hbm, site_hbm, pos_hbm, chan_hbm, atten_hbm,
                 mine_ref, theirs_ref, send_ref, mask_ref, src_ref, site_ref, pos_ref, chan_ref, atten_ref,
                 spec, travel, source, small_sems, sems):
    ev_n, freqs, ch_n = spec_hbm.shape
    half = ch_n // 2
    half_tiles = half // TILE
    core = core_index()
    small = []
    for i, (src, dst) in enumerate((
            (pos_hbm, pos_ref), (chan_hbm, chan_ref), (mask_hbm, mask_ref),
            (atten_hbm, atten_ref), (src_hbm, src_ref), (site_hbm, site_ref))):
        copy = pltpu.make_async_copy(src, dst, small_sems.at[i])
        copy.start()
        small.append(copy)
    copies = []
    for e in range(ev_n):
        copy = pltpu.make_async_copy(spec_hbm.at[e], spec.at[e], sems.at[e])
        copy.start()
        copies.append(copy)
    for copy in small:
        copy.wait()
    maskf = mask_ref[...].astype(F32)
    low, high = maskf[:, :half_tiles], maskf[:, half_tiles:]
    upper = core == 1
    for ref, own in ((mine_ref, True), (theirs_ref, False)):
        first, second = (high, low) if own else (low, high)
        picked = jnp.where(upper, first, second)
        for t in range(half_tiles):
            ref[ev_n, :, t * TILE:(t + 1) * TILE] = jnp.broadcast_to(picked[:, t:t + 1], (ev_n, TILE))
    count = jnp.sum(jnp.sum(maskf, axis=1, keepdims=True), axis=0, keepdims=True) * float(TILE)
    cols = [jnp.broadcast_to(as_column(widen(pos_ref[k:k + 1, :]), ev_n), (ev_n, TILE)) for k in range(3)]

    def travel_step(t, _):
        at = tile_at(t)
        east = cols[0] - chan_ref[0:1, at]
        north = cols[1] - chan_ref[1:2, at]
        travel[:, at] = jnp.sqrt(east * east + north * north + cols[2] * cols[2]) / 3.0
        return 0
    lax.fori_loop(0, ch_n // TILE, travel_step, 0, unroll=4)
    att = jnp.broadcast_to(as_column(widen(atten_ref[...]), freqs), (freqs, TILE))
    for e in range(ev_n):
        source[e] = jnp.broadcast_to(as_column(widen(src_ref[e:e + 1, :]), freqs), (freqs, TILE))
    total = jnp.zeros((freqs, TILE), F32)
    for e in range(ev_n):
        copies[e].wait()
        src = source[e]
        for ref, own in ((mine_ref, True), (theirs_ref, False)):
            base = (core if own else 1 - core) * half_tiles

            def step(t, acc, ref=ref, base=base, e=e, src=src):
                here, at = tile_at(t), tile_at(base + t)
                time = jnp.broadcast_to(travel[e:e + 1, at], (freqs, TILE))
                resid = (spec[e, :, at] - src) + (att * time - site_ref[:, at])
                ref[e, :, here] = resid
                valid = jnp.broadcast_to(ref[ev_n, e:e + 1, here], (freqs, TILE))
                return acc + jnp.abs(resid) * valid
            total = lax.fori_loop(0, half_tiles, step, total, unroll=8)
    row = as_row(jnp.sum(total, axis=1, keepdims=True))
    lane = lax.broadcasted_iota(jnp.int32, row.shape, 1)
    row = row + jnp.where(lane == freqs, jnp.broadcast_to(count, row.shape), 0.0)
    send_ref[...] = jnp.broadcast_to(row, send_ref.shape)


def weight_kernel(freqs, total_ref, count_ref, mine_ref, theirs_ref, a_ref, b_ref, src_ref):
    ev_n = mine_ref.shape[0] - 1
    half = mine_ref.shape[2]
    quarter = half // 2
    core = core_index()
    row = jnp.sum(total_ref[...], axis=0, keepdims=True)
    counts = jnp.sum(count_ref[...], axis=0, keepdims=True)
    lane = lax.broadcasted_iota(jnp.int32, row.shape, 1)
    count = jnp.sum(jnp.where(lane == freqs, counts, 0.0), axis=1, keepdims=True)
    delta = 1.345 * (1.2533 * row / jnp.maximum(count, 1.0) + 1e-05)
    delta = jnp.broadcast_to(as_column(delta, freqs), (freqs, TILE))
    per_row = LANES // freqs
    zero = jnp.zeros((freqs, TILE), F32)
    a_ref[...] = jnp.zeros_like(a_ref)
    b_ref[...] = jnp.zeros_like(b_ref)
    for which, ref in enumerate((mine_ref, theirs_ref)):
        owner = core if which == 0 else 1 - core
        nums, dens = [], []
        for start in range(0, ev_n, GROUP):
            events = range(start, start + GROUP)

            def step(t, acc, ref=ref, events=events):
                acc = list(acc)
                for out, base in ((a_ref, 0), (b_ref, quarter // TILE)):
                    here, at = tile_at(t), tile_at(base + t)
                    num, den = out[0, :, here], out[1, :, here]
                    for k, e in enumerate(events):
                        resid = ref[e, :, at]
                        valid = jnp.broadcast_to(ref[ev_n, e:e + 1, at], (freqs, TILE))
                        weight = valid * delta / jnp.maximum(jnp.abs(resid), delta)
                        product = weight * resid
                        num, den = num + product, den + weight
                        acc[2 * k] += product
                        acc[2 * k + 1] += weight
                    out[0, :, here] = num
                    out[1, :, here] = den
                return tuple(acc)
            acc = lax.fori_loop(0, quarter // TILE, step, (zero,) * (2 * GROUP))
            nums += acc[0::2]
            dens += acc[1::2]
        rows_each = ev_n // per_row
        for kind, parts in ((0, nums), (1, dens)):
            for i in range(rows_each):
                block = jnp.concatenate(parts[i * per_row:(i + 1) * per_row], axis=0)
                line = jnp.sum(block.T, axis=0, keepdims=True)
                src_ref[pl.ds(kind * 2 * rows_each + owner * rows_each + i, 1), :] = line


def increments(src_a, src_b):
    sums = src_a + src_b
    rows = sums.shape[0] // 2
    return 0.5 * sums[:rows] / (sums[rows:] + 1.0)


def site_increment(refs, at):
    num = refs[0][0, :, at] + refs[1][0, :, at]
    den = refs[0][1, :, at] + refs[1][1, :, at]
    return 0.5 * num / (den + 1.0)


def update_kernel(a0, a1, b0, b1, s0, s1, mine_ref, theirs_ref,
                  new_mine, new_theirs, dsite_ref, dsrc_ref, send_ref, shift):
    ev_n = mine_ref.shape[0] - 1
    freqs, half = mine_ref.shape[1:]
    quarter = half // 2
    core = core_index()
    dsrc = increments(s0[...], s1[...])
    dsrc_ref[...] = dsrc
    for i in range(dsrc.shape[0]):
        shift[i * LANES:(i + 1) * LANES, :] = jnp.broadcast_to(dsrc[i:i + 1, :], (LANES, LANES)).T
    for refs, base in (((a0, a1), 0), ((b0, b1), quarter // TILE)):
        for t in range(quarter // TILE):
            at = slice(t * TILE, (t + 1) * TILE)
            there = slice((base + t) * TILE, (base + t + 1) * TILE)
            dsite_ref[:, there] = site_increment(refs, at)
    total = jnp.zeros((freqs, TILE), F32)
    for which, (ref, out) in enumerate(((mine_ref, new_mine), (theirs_ref, new_theirs))):
        owner = core if which == 0 else 1 - core
        out[ev_n] = ref[ev_n]
        for e in range(ev_n):
            first = pl.multiple_of((owner * ev_n + e) * freqs, freqs)
            src = shift[pl.ds(first, freqs), :]

            def step(t, acc, ref=ref, out=out, e=e, src=src):
                at = tile_at(t)
                resid = ref[e, :, at] - src - dsite_ref[:, at]
                out[e, :, at] = resid
                valid = jnp.broadcast_to(ref[ev_n, e:e + 1, at], (freqs, TILE))
                return acc + jnp.abs(resid) * valid
            total = lax.fori_loop(0, half // TILE, step, total, unroll=8)
    row = as_row(jnp.sum(total, axis=1, keepdims=True))
    send_ref[...] = jnp.broadcast_to(row, send_ref.shape)


def site_kernel(a0, a1, b0, b1, s0, s1, site_ref, dsite_ref, dsrc_ref,
                new_ref, src_ref, send_ref):
    freqs, half = dsite_ref.shape
    quarter = half // 2
    core = core_index()
    src_ref[...] = dsrc_ref[...] + increments(s0[...], s1[...])
    total = jnp.zeros((freqs, TILE), F32)
    for refs, base in (((a0, a1), 0), ((b0, b1), quarter // TILE)):
        for t in range(quarter // TILE):
            at = slice(t * TILE, (t + 1) * TILE)
            there = slice((base + t) * TILE, (base + t + 1) * TILE)
            init = site_ref[:, tile_at(core * (half // TILE) + base + t)]
            value = init + dsite_ref[:, there] + site_increment(refs, at)
            new_ref[:, there] = value
            total = total + value
    row = as_row(jnp.sum(total, axis=1, keepdims=True))
    send_ref[...] = jnp.broadcast_to(row, send_ref.shape)


def finish_kernel(total_ch, sums_ref, mine_ref, theirs_ref, source_ref, out_source, out_site):
    freqs, half = mine_ref.shape
    core = core_index()
    row = jnp.sum(sums_ref[...], axis=0, keepdims=True) / total_ch
    column = jnp.broadcast_to(as_column(row, freqs), (freqs, TILE))
    out_source[...] = source_ref[...] + row[:, :freqs]
    for ref, owner in ((mine_ref, core), (theirs_ref, 1 - core)):
        for t in range(half // TILE):
            at = tile_at(owner * (half // TILE) + t)
            out_site[:, at] = ref[:, t * TILE:(t + 1) * TILE] - column


def call(kernel, out_shape, in_specs, scratch=()):
    outs = [jax.ShapeDtypeStruct(shape, F32) for shape in out_shape]
    return pl.pallas_call(
        kernel,
        out_shape=outs,
        in_specs=in_specs,
        out_specs=[VMEM] * len(outs),
        scratch_shapes=list(scratch),
        compiler_params=pltpu.CompilerParams(vmem_limit_bytes=LIMIT),
    )


def swap(value, axis, size, bit):
    return lax.ppermute(value, axis, [(i, i ^ bit) for i in range(size)])


def on_device(spectra, tile_mask, source_init, site_init, event_pos, channel_pos, atten):
    ev_n, freqs, ch_n = spectra.shape
    ev_dev, ch_dev = lax.axis_size("ev"), lax.axis_size("ch")
    devices = ev_dev * ch_dev
    half, quarter = ch_n // 2, ch_n // 4
    slabs = (ev_n + 1, freqs, half)
    src_rows = 2 * ev_n * freqs // LANES
    ev_bits = [1 << k for k in range(1, ev_dev.bit_length() - 1)]
    ch_bits = [1 << k for k in range(ch_dev.bit_length() - 1)]
    pairs = [[(2 * g + c) * ch_dev + z for c in range(2) for z in range(ch_dev)] for g in range(ev_dev // 2)]

    inputs = [pltpu.with_memory_space_constraint(x, pltpu.HBM) for x in (
        spectra, tile_mask, source_init, site_init, event_pos, channel_pos, atten.reshape(1, freqs))]
    small = inputs[1:]
    mine, theirs, sums = call(
        resid_kernel, [slabs, slabs, (devices, LANES)], [HBM] * 7,
        [pltpu.VMEM(x.shape, x.dtype) for x in small]
        + [pltpu.VMEM(spectra.shape, F32), pltpu.VMEM((ev_n, ch_n), F32),
           pltpu.VMEM((ev_n, freqs, TILE), F32), pltpu.SemaphoreType.DMA((len(small),)),
           pltpu.SemaphoreType.DMA((ev_n,))],
    )(*inputs)
    theirs = swap(theirs, "ev", ev_dev, 1)
    first = None
    for step in range(ITERS):
        total = lax.all_to_all(sums, ("ev", "ch"), 0, 0)
        first = total if first is None else first
        a, b, src = call(
            functools.partial(weight_kernel, freqs),
            [(2, freqs, quarter), (2, freqs, quarter), (2 * src_rows, LANES)], [VMEM] * 4,
        )(total, first, mine, theirs)
        src = src + swap(src, "ev", ev_dev, 1)
        src_other = jnp.zeros_like(src)
        for k in range(max(len(ev_bits), len(ch_bits))):
            if k > 0:
                a_sum, b_sum, src_sum = a, b, src
                if k < len(ev_bits):
                    a_sum, b_sum = a + a_other, b + b_other
                if k < len(ch_bits):
                    src_sum = src + src_other
                a, b, src = lax.optimization_barrier((a_sum, b_sum, src_sum))
            if k < len(ev_bits):
                a_other = swap(a, "ev", ev_dev, ev_bits[k])
                b_other = swap(b, "ev", ev_dev, ev_bits[(k + len(ev_bits) // 2) % len(ev_bits)])
            if k < len(ch_bits):
                src_other = swap(src, "ch", ch_dev, ch_bits[k])
        parts = (a, a_other, b, b_other, src, src_other)
        if step < ITERS - 1:
            mine, theirs, dsite, dsrc, sums = call(
                update_kernel, [slabs, slabs, (freqs, half), (src_rows, LANES), (devices, LANES)], [VMEM] * 8,
                [pltpu.VMEM((src_rows * LANES, LANES), F32)],
            )(*parts, mine, theirs)
    site, dsrc, sums = call(
        site_kernel, [(freqs, half), (src_rows, LANES), (2 * ch_dev, LANES)], [VMEM] * 9,
    )(*parts, site_init, dsite, dsrc)
    site_other = swap(site, "ev", ev_dev, 1)
    sums = lax.all_to_all(sums, ("ev", "ch"), 0, 0, axis_index_groups=pairs)
    core = lax.rem(lax.axis_index("ev"), 2)
    own = lax.dynamic_slice(dsrc, (core * (src_rows // 2), 0), (src_rows // 2, LANES))
    source = source_init + own.reshape(ev_n, freqs)
    return tuple(call(
        functools.partial(finish_kernel, float(ch_n * ch_dev)), [(ev_n, freqs), (freqs, ch_n)], [VMEM] * 4,
    )(sums, site, site_other, source))


def solution(mesh):
    in_specs = (
        P("ev", None, "ch"),
        P("ev", "ch"),
        P("ev", None),
        P(None, "ch"),
        P(None, "ev"),
        P(None, "ch"),
        P(),
    )
    out_specs = (P("ev", None), P(None, "ch"))
    return jax.shard_map(
        on_device, mesh=mesh, in_specs=in_specs, out_specs=out_specs, check_vma=False
    )
```

```python
import functools

import jax
import jax.numpy as jnp
from jax import lax
from jax.experimental import pallas as pl
from jax.experimental.pallas import tpu as pltpu
from jax.sharding import PartitionSpec as P

ITERS = 2
LANES = 128
TILE = 128
GROUP = 4
CHAINS = 4
BATCH = 4
F32 = jnp.float32
VMEM = pl.BlockSpec(memory_space=pltpu.VMEM)
HBM = pl.BlockSpec(memory_space=pltpu.HBM)
LIMIT = 24 * 1024 * 1024


def eye(rows):
    shape = (rows, LANES)
    return lax.broadcasted_iota(jnp.int32, shape, 0) == lax.broadcasted_iota(jnp.int32, shape, 1)


def as_column(row, rows):
    spread = jnp.where(eye(rows), jnp.broadcast_to(row, (rows, LANES)), 0.0)
    return jnp.sum(spread, axis=1, keepdims=True)


def as_row(column):
    rows = column.shape[0]
    spread = jnp.where(eye(rows), jnp.broadcast_to(column, (rows, LANES)), 0.0)
    return jnp.sum(spread, axis=0, keepdims=True)


def widen(row):
    return jnp.concatenate([row, jnp.zeros((1, LANES - row.shape[1]), F32)], axis=1)


def tile_at(index):
    return pl.ds(pl.multiple_of(index * TILE, TILE), TILE)


def core_index():
    return lax.rem(lax.axis_index("ev"), 2)


def resid_kernel(spec_hbm, mask_hbm, src_hbm, site_hbm, pos_hbm, chan_hbm, atten_hbm,
                 mine_ref, theirs_ref, send_ref, mask_ref, src_ref, site_ref, pos_ref, chan_ref, atten_ref,
                 spec, travel, source, small_sems, sems):
    ev_n, freqs, ch_n = spec_hbm.shape
    half = ch_n // 2
    half_tiles = half // TILE
    core = core_index()
    small = []
    for i, (src, dst) in enumerate((
            (pos_hbm, pos_ref), (chan_hbm, chan_ref), (mask_hbm, mask_ref),
            (atten_hbm, atten_ref), (src_hbm, src_ref), (site_hbm, site_ref))):
        copy = pltpu.make_async_copy(src, dst, small_sems.at[i])
        copy.start()
        small.append(copy)
    copies = [pltpu.make_async_copy(spec_hbm.at[e], spec.at[e], sems.at[e]) for e in range(ev_n)]
    for copy in copies[:4]:
        copy.start()
    for copy in small:
        copy.wait()
    for copy in copies[4:]:
        copy.start()
    maskf = mask_ref[...].astype(F32)
    low, high = maskf[:, :half_tiles], maskf[:, half_tiles:]
    upper = core == 1
    for ref, own in ((mine_ref, True), (theirs_ref, False)):
        first, second = (high, low) if own else (low, high)
        picked = jnp.where(upper, first, second)
        for t in range(half_tiles):
            ref[ev_n, :, t * TILE:(t + 1) * TILE] = jnp.broadcast_to(picked[:, t:t + 1], (ev_n, TILE))
    count = jnp.sum(jnp.sum(maskf, axis=1, keepdims=True), axis=0, keepdims=True) * float(TILE)
    cols = [jnp.broadcast_to(as_column(widen(pos_ref[k:k + 1, :]), ev_n), (ev_n, TILE)) for k in range(3)]

    def travel_step(t, _):
        at = tile_at(t)
        east = cols[0] - chan_ref[0:1, at]
        north = cols[1] - chan_ref[1:2, at]
        travel[:, at] = jnp.sqrt(east * east + north * north + cols[2] * cols[2]) / 3.0
        return 0
    lax.fori_loop(0, ch_n // TILE, travel_step, 0, unroll=4)
    att = jnp.broadcast_to(as_column(widen(atten_ref[...]), freqs), (freqs, TILE))
    for e in range(ev_n):
        source[e] = jnp.broadcast_to(as_column(widen(src_ref[e:e + 1, :]), freqs), (freqs, TILE))
    totals = (jnp.zeros((freqs, TILE), F32),) * CHAINS
    for start in range(0, ev_n, BATCH):
        events = range(start, start + BATCH)
        for e in events:
            copies[e].wait()

        def step(t, totals, events=events):
            totals = list(totals)
            here = tile_at(t)
            for ref, own in ((mine_ref, True), (theirs_ref, False)):
                at = tile_at((core if own else 1 - core) * half_tiles + t)
                site = site_ref[:, at]
                for k, e in enumerate(events):
                    time = jnp.broadcast_to(travel[e:e + 1, at], (freqs, TILE))
                    resid = (spec[e, :, at] - source[e]) + (att * time - site)
                    ref[e, :, here] = resid
                    valid = jnp.broadcast_to(ref[ev_n, e:e + 1, here], (freqs, TILE))
                    totals[k % CHAINS] += jnp.abs(resid) * valid
            return tuple(totals)
        totals = lax.fori_loop(0, half_tiles, step, totals, unroll=2)
    total = sum(totals[1:], totals[0])
    row = as_row(jnp.sum(total, axis=1, keepdims=True))
    lane = lax.broadcasted_iota(jnp.int32, row.shape, 1)
    row = row + jnp.where(lane == freqs, jnp.broadcast_to(count, row.shape), 0.0)
    send_ref[...] = jnp.broadcast_to(row, send_ref.shape)


def weight_kernel(freqs, total_ref, count_ref, mine_ref, theirs_ref, a_ref, b_ref, src_ref):
    ev_n = mine_ref.shape[0] - 1
    half = mine_ref.shape[2]
    quarter = half // 2
    core = core_index()
    row = jnp.sum(total_ref[...], axis=0, keepdims=True)
    counts = jnp.sum(count_ref[...], axis=0, keepdims=True)
    lane = lax.broadcasted_iota(jnp.int32, row.shape, 1)
    count = jnp.sum(jnp.where(lane == freqs, counts, 0.0), axis=1, keepdims=True)
    delta = 1.345 * (1.2533 * row / jnp.maximum(count, 1.0) + 1e-05)
    delta = jnp.broadcast_to(as_column(delta, freqs), (freqs, TILE))
    per_row = LANES // freqs
    zero = jnp.zeros((freqs, TILE), F32)
    a_ref[...] = jnp.zeros_like(a_ref)
    b_ref[...] = jnp.zeros_like(b_ref)
    for which, ref in enumerate((mine_ref, theirs_ref)):
        owner = core if which == 0 else 1 - core
        final = which == 1
        nums, dens = [], []
        for start in range(0, ev_n, GROUP):
            events = range(start, start + GROUP)
            scale = final and start + GROUP >= ev_n

            def step(t, acc, ref=ref, events=events, scale=scale):
                acc = list(acc)
                for out, base in ((a_ref, 0), (b_ref, quarter // TILE)):
                    here, at = tile_at(t), tile_at(base + t)
                    num, den = out[0, :, here], out[1, :, here]
                    for k, e in enumerate(events):
                        resid = ref[e, :, at]
                        valid = jnp.broadcast_to(ref[ev_n, e:e + 1, at], (freqs, TILE))
                        weight = pl.reciprocal(jnp.maximum(jnp.abs(resid), delta), approx=True) * valid
                        product = weight * resid
                        num, den = num + product, den + weight
                        acc[2 * k] += product
                        acc[2 * k + 1] += weight
                    if scale:
                        num, den = num * delta, den * delta
                    out[0, :, here] = num
                    out[1, :, here] = den
                return tuple(acc)
            acc = lax.fori_loop(0, quarter // TILE, step, (zero,) * (2 * GROUP), unroll=8)
            nums += [x * delta for x in acc[0::2]]
            dens += [x * delta for x in acc[1::2]]
        rows_each = ev_n // per_row
        for kind, parts in ((0, nums), (1, dens)):
            for i in range(rows_each):
                block = jnp.concatenate(parts[i * per_row:(i + 1) * per_row], axis=0)
                line = jnp.sum(block.T, axis=0, keepdims=True)
                at_row = kind * 2 * rows_each + owner * rows_each + i
                for copy in range(src_ref.shape[0]):
                    src_ref[copy, pl.ds(at_row, 1), :] = line


def increments(num, den):
    return 0.5 * num / (den + 1.0)


def site_increment(refs, at):
    num = refs[0][0, :, at] + refs[1][0, :, at]
    den = refs[0][1, :, at] + refs[1][1, :, at]
    return increments(num, den)


def update_kernel(a0, a1, b0, b1, sums_ref, mine_ref, theirs_ref,
                  new_mine, new_theirs, dsite_ref, dsrc_ref, send_ref, shift):
    ev_n = mine_ref.shape[0] - 1
    freqs, half = mine_ref.shape[1:]
    quarter = half // 2
    core = core_index()
    sums = jnp.sum(sums_ref[...], axis=0)
    rows = dsrc_ref.shape[0]
    dsrc = increments(sums[:rows], sums[rows:])
    dsrc_ref[...] = dsrc
    for i in range(dsrc.shape[0]):
        shift[i * LANES:(i + 1) * LANES, :] = jnp.broadcast_to(dsrc[i:i + 1, :], (LANES, LANES)).T
    for refs, base in (((a0, a1), 0), ((b0, b1), quarter // TILE)):
        for t in range(quarter // TILE):
            at = slice(t * TILE, (t + 1) * TILE)
            there = slice((base + t) * TILE, (base + t + 1) * TILE)
            dsite_ref[:, there] = site_increment(refs, at)
    totals = (jnp.zeros((freqs, TILE), F32),) * CHAINS
    for which, (ref, out) in enumerate(((mine_ref, new_mine), (theirs_ref, new_theirs))):
        owner = core if which == 0 else 1 - core
        out[ev_n] = ref[ev_n]

        def step(t, totals, ref=ref, out=out, owner=owner):
            totals = list(totals)
            at = tile_at(t)
            site = dsite_ref[:, at]
            for e in range(ev_n):
                src = shift[pl.ds(pl.multiple_of((owner * ev_n + e) * freqs, freqs), freqs), :]
                resid = (ref[e, :, at] - src) - site
                out[e, :, at] = resid
                valid = jnp.broadcast_to(ref[ev_n, e:e + 1, at], (freqs, TILE))
                totals[e % CHAINS] += jnp.abs(resid) * valid
            return tuple(totals)
        totals = lax.fori_loop(0, half // TILE, step, totals, unroll=2)
    total = sum(totals[1:], totals[0])
    row = as_row(jnp.sum(total, axis=1, keepdims=True))
    send_ref[...] = jnp.broadcast_to(row, send_ref.shape)


def site_kernel(a0, a1, b0, b1, src_ref, site_ref, dsite_ref, new_ref, send_ref):
    freqs, half = dsite_ref.shape
    quarter = half // 2
    core = core_index()
    total = jnp.zeros((freqs, TILE), F32)
    for refs, base in (((a0, a1), 0), ((b0, b1), quarter // TILE)):
        for t in range(quarter // TILE):
            at = slice(t * TILE, (t + 1) * TILE)
            there = slice((base + t) * TILE, (base + t + 1) * TILE)
            init = site_ref[:, tile_at(core * (half // TILE) + base + t)]
            value = init + dsite_ref[:, there] + site_increment(refs, at)
            new_ref[:, there] = value
            total = total + value
    row = as_row(jnp.sum(total, axis=1, keepdims=True))
    rows = src_ref.shape[1] // 4
    count = send_ref.shape[0] // 2
    for owner in range(2):
        parts = [src_ref[0, (2 * kind + owner) * rows:(2 * kind + owner + 1) * rows, :] for kind in range(2)]
        pad = jnp.zeros((send_ref.shape[1] - 2 * rows - 1, LANES), F32)
        block = jnp.concatenate(parts + [row, pad], axis=0)
        for copy in range(count):
            send_ref[owner * count + copy] = block


def finish_kernel(total_ch, sums_ref, mine_ref, theirs_ref, dsrc_ref, source_ref, out_source, out_site):
    freqs, half = mine_ref.shape
    core = core_index()
    sums = jnp.sum(sums_ref[...], axis=0)
    rows = dsrc_ref.shape[0] // 2
    row = sums[2 * rows:2 * rows + 1] / total_ch
    column = jnp.broadcast_to(as_column(row, freqs), (freqs, TILE))
    for ref, owner in ((mine_ref, core), (theirs_ref, 1 - core)):
        for t in range(half // TILE):
            at = tile_at(owner * (half // TILE) + t)
            out_site[:, at] = ref[:, t * TILE:(t + 1) * TILE] - column
    change = dsrc_ref[pl.ds(core * rows, rows), :] + increments(sums[:rows], sums[rows:2 * rows])
    per_row = LANES // freqs
    for e in range(source_ref.shape[0]):
        first = (e % per_row) * freqs
        piece = change[e // per_row:e // per_row + 1, first:first + freqs]
        out_source[e:e + 1, :] = source_ref[e:e + 1, :] + piece + row[:, :freqs]


def call(kernel, out_shape, in_specs, scratch=()):
    outs = [jax.ShapeDtypeStruct(shape, F32) for shape in out_shape]
    return pl.pallas_call(
        kernel,
        out_shape=outs,
        in_specs=in_specs,
        out_specs=[VMEM] * len(outs),
        scratch_shapes=list(scratch),
        compiler_params=pltpu.CompilerParams(vmem_limit_bytes=LIMIT),
    )


def swap(value, axis, size, bit):
    return lax.ppermute(value, axis, [(i, i ^ bit) for i in range(size)])


def on_device(spectra, tile_mask, source_init, site_init, event_pos, channel_pos, atten):
    ev_n, freqs, ch_n = spectra.shape
    ev_dev, ch_dev = lax.axis_size("ev"), lax.axis_size("ch")
    devices = ev_dev * ch_dev
    half, quarter = ch_n // 2, ch_n // 4
    slabs = (ev_n + 1, freqs, half)
    src_rows = 2 * ev_n * freqs // LANES
    ev_bits = [1 << k for k in range(1, ev_dev.bit_length() - 1)]
    ch_bits = [1 << k for k in range(ch_dev.bit_length() - 1)]
    pairs = [[(2 * g + c) * ch_dev + z for c in range(2) for z in range(ch_dev)] for g in range(ev_dev // 2)]

    inputs = [pltpu.with_memory_space_constraint(x, pltpu.HBM) for x in (
        spectra, tile_mask, source_init, site_init, event_pos, channel_pos, atten.reshape(1, freqs))]
    small = inputs[1:]
    mine, theirs, sums = call(
        resid_kernel, [slabs, slabs, (devices, LANES)], [HBM] * 7,
        [pltpu.VMEM(x.shape, x.dtype) for x in small]
        + [pltpu.VMEM(spectra.shape, F32), pltpu.VMEM((ev_n, ch_n), F32),
           pltpu.VMEM((ev_n, freqs, TILE), F32), pltpu.SemaphoreType.DMA((len(small),)),
           pltpu.SemaphoreType.DMA((ev_n,))],
    )(*inputs)
    theirs = swap(theirs, "ev", ev_dev, 1)
    first = None
    for step in range(ITERS):
        last = step == ITERS - 1
        total = lax.all_to_all(sums, ("ev", "ch"), 0, 0)
        first = total if first is None else first
        a, b, src = call(
            functools.partial(weight_kernel, freqs),
            [(2, freqs, quarter), (2, freqs, quarter), (1, 2 * src_rows, LANES)],
            [VMEM] * 4,
        )(total, first, mine, theirs)
        if not last:
            src = src + swap(src, "ev", ev_dev, 1)
        for k in range(max(len(ev_bits), len(ch_bits))):
            if k > 0:
                if k < len(ev_bits):
                    a, b = a + a_other, b + b_other
                if not last and k <= len(ch_bits):
                    src = src + src_other
                    a, b, _ = lax.optimization_barrier((a, b, src))
            if k < len(ev_bits):
                a_other = swap(a, "ev", ev_dev, ev_bits[k])
                b_other = swap(b, "ev", ev_dev, ev_bits[(k + len(ev_bits) // 2) % len(ev_bits)])
            if not last and k < len(ch_bits):
                src_other = swap(src, "ch", ch_dev, ch_bits[k])
        if not last:
            src = src + src_other
        parts = (a, a_other, b, b_other, src)
        if not last:
            mine, theirs, dsite, dsrc, sums = call(
                update_kernel, [slabs, slabs, (freqs, half), (src_rows, LANES), (devices, LANES)], [VMEM] * 7,
                [pltpu.VMEM((src_rows * LANES, LANES), F32)],
            )(*parts, mine, theirs)
    site, sums = call(
        site_kernel, [(freqs, half), (len(pairs[0]), 8, LANES)], [VMEM] * 7,
    )(*parts, site_init, dsite)
    site_other = swap(site, "ev", ev_dev, 1)
    sums = lax.all_to_all(sums, ("ev", "ch"), 0, 0, axis_index_groups=pairs)
    return tuple(call(
        functools.partial(finish_kernel, float(ch_n * ch_dev)), [(ev_n, freqs), (freqs, ch_n)], [VMEM] * 5,
    )(sums, site, site_other, dsrc, source_init))


def solution(mesh):
    in_specs = (
        P("ev", None, "ch"),
        P("ev", "ch"),
        P("ev", None),
        P(None, "ch"),
        P(None, "ev"),
        P(None, "ch"),
        P(),
    )
    out_specs = (P("ev", None), P(None, "ch"))
    return jax.shard_map(
        on_device, mesh=mesh, in_specs=in_specs, out_specs=out_specs, check_vma=False
    )
```

```python
import functools

import jax
import jax.numpy as jnp
from jax import lax
from jax.experimental import pallas as pl
from jax.experimental.pallas import tpu as pltpu
from jax.sharding import PartitionSpec as P

ITERS = 2
LANES = 128
TILE = 128
GROUP = 4
CHAINS = 4
BATCH = 4
F32 = jnp.float32
VMEM = pl.BlockSpec(memory_space=pltpu.VMEM)
HBM = pl.BlockSpec(memory_space=pltpu.HBM)
LIMIT = 24 * 1024 * 1024


def eye(rows):
    shape = (rows, LANES)
    return lax.broadcasted_iota(jnp.int32, shape, 0) == lax.broadcasted_iota(jnp.int32, shape, 1)


def as_column(row, rows):
    spread = jnp.where(eye(rows), jnp.broadcast_to(row, (rows, LANES)), 0.0)
    return jnp.sum(spread, axis=1, keepdims=True)


def as_row(column):
    rows = column.shape[0]
    spread = jnp.where(eye(rows), jnp.broadcast_to(column, (rows, LANES)), 0.0)
    return jnp.sum(spread, axis=0, keepdims=True)


def widen(row):
    return jnp.concatenate([row, jnp.zeros((1, LANES - row.shape[1]), F32)], axis=1)


def tile_at(index):
    return pl.ds(pl.multiple_of(index * TILE, TILE), TILE)


def core_index():
    return lax.rem(lax.axis_index("ev"), 2)


def resid_kernel(spec_hbm, mask_hbm, src_hbm, site_hbm, pos_hbm, chan_hbm, atten_hbm,
                 mine_ref, theirs_ref, send_ref, mask_ref, src_ref, site_ref, pos_ref, chan_ref, atten_ref,
                 spec, travel, source, small_sems, sems):
    ev_n, freqs, ch_n = spec_hbm.shape
    half = ch_n // 2
    half_tiles = half // TILE
    core = core_index()
    small = []
    for i, (src, dst) in enumerate((
            (pos_hbm, pos_ref), (chan_hbm, chan_ref), (mask_hbm, mask_ref),
            (atten_hbm, atten_ref), (src_hbm, src_ref), (site_hbm, site_ref))):
        copy = pltpu.make_async_copy(src, dst, small_sems.at[i])
        copy.start()
        small.append(copy)
    copies = [pltpu.make_async_copy(spec_hbm.at[e], spec.at[e], sems.at[e]) for e in range(ev_n)]
    for copy in copies[:4]:
        copy.start()
    for copy in small:
        copy.wait()
    for copy in copies[4:]:
        copy.start()
    maskf = mask_ref[...].astype(F32)
    low, high = maskf[:, :half_tiles], maskf[:, half_tiles:]
    upper = core == 1
    for ref, own in ((mine_ref, True), (theirs_ref, False)):
        first, second = (high, low) if own else (low, high)
        picked = jnp.where(upper, first, second)
        for t in range(half_tiles):
            ref[ev_n, :, t * TILE:(t + 1) * TILE] = jnp.broadcast_to(picked[:, t:t + 1], (ev_n, TILE))
    count = jnp.sum(jnp.sum(maskf, axis=1, keepdims=True), axis=0, keepdims=True) * float(TILE)
    cols = [jnp.broadcast_to(as_column(widen(pos_ref[k:k + 1, :]), ev_n), (ev_n, TILE)) for k in range(3)]

    def travel_step(t, _):
        at = tile_at(t)
        east = cols[0] - chan_ref[0:1, at]
        north = cols[1] - chan_ref[1:2, at]
        travel[:, at] = jnp.sqrt(east * east + north * north + cols[2] * cols[2]) / 3.0
        return 0
    lax.fori_loop(0, ch_n // TILE, travel_step, 0, unroll=4)
    att = jnp.broadcast_to(as_column(widen(atten_ref[...]), freqs), (freqs, TILE))
    for e in range(ev_n):
        source[e] = jnp.broadcast_to(as_column(widen(src_ref[e:e + 1, :]), freqs), (freqs, TILE))
    totals = (jnp.zeros((freqs, TILE), F32),) * CHAINS
    for start in range(0, ev_n, BATCH):
        events = range(start, start + BATCH)
        for e in events:
            copies[e].wait()

        def step(t, totals, events=events):
            totals = list(totals)
            here = tile_at(t)
            for ref, own in ((mine_ref, True), (theirs_ref, False)):
                at = tile_at((core if own else 1 - core) * half_tiles + t)
                site = site_ref[:, at]
                for k, e in enumerate(events):
                    time = jnp.broadcast_to(travel[e:e + 1, at], (freqs, TILE))
                    resid = (spec[e, :, at] - source[e]) + (att * time - site)
                    ref[e, :, here] = resid
                    valid = jnp.broadcast_to(ref[ev_n, e:e + 1, here], (freqs, TILE))
                    totals[k % CHAINS] += jnp.abs(resid) * valid
            return tuple(totals)
        totals = lax.fori_loop(0, half_tiles, step, totals, unroll=2)
    total = sum(totals[1:], totals[0])
    row = as_row(jnp.sum(total, axis=1, keepdims=True))
    lane = lax.broadcasted_iota(jnp.int32, row.shape, 1)
    row = row + jnp.where(lane == freqs, jnp.broadcast_to(count, row.shape), 0.0)
    send_ref[...] = jnp.broadcast_to(row, send_ref.shape)


def weight_kernel(freqs, total_ref, count_ref, mine_ref, theirs_ref, a_ref, b_ref, src_ref):
    ev_n = mine_ref.shape[0] - 1
    half = mine_ref.shape[2]
    quarter = half // 2
    core = core_index()
    row = jnp.sum(total_ref[...], axis=0, keepdims=True)
    counts = jnp.sum(count_ref[...], axis=0, keepdims=True)
    lane = lax.broadcasted_iota(jnp.int32, row.shape, 1)
    count = jnp.sum(jnp.where(lane == freqs, counts, 0.0), axis=1, keepdims=True)
    delta = 1.345 * (1.2533 * row / jnp.maximum(count, 1.0) + 1e-05)
    delta = jnp.broadcast_to(as_column(delta, freqs), (freqs, TILE))
    per_row = LANES // freqs
    zero = jnp.zeros((freqs, TILE), F32)
    a_ref[...] = jnp.zeros_like(a_ref)
    b_ref[...] = jnp.zeros_like(b_ref)
    for which, ref in enumerate((mine_ref, theirs_ref)):
        owner = core if which == 0 else 1 - core
        final = which == 1
        nums, dens = [], []
        for start in range(0, ev_n, GROUP):
            events = range(start, start + GROUP)
            scale = final and start + GROUP >= ev_n

            def step(t, acc, ref=ref, events=events, scale=scale):
                acc = list(acc)
                for out, base in ((a_ref, 0), (b_ref, quarter // TILE)):
                    here, at = tile_at(t), tile_at(base + t)
                    num, den = out[0, :, here], out[1, :, here]
                    for k, e in enumerate(events):
                        resid = ref[e, :, at]
                        valid = jnp.broadcast_to(ref[ev_n, e:e + 1, at], (freqs, TILE))
                        weight = pl.reciprocal(jnp.maximum(jnp.abs(resid), delta), approx=True) * valid
                        product = weight * resid
                        num, den = num + product, den + weight
                        acc[2 * k] += product
                        acc[2 * k + 1] += weight
                    if scale:
                        num, den = num * delta, den * delta
                    out[0, :, here] = num
                    out[1, :, here] = den
                return tuple(acc)
            acc = lax.fori_loop(0, quarter // TILE, step, (zero,) * (2 * GROUP), unroll=8)
            nums += [x * delta for x in acc[0::2]]
            dens += [x * delta for x in acc[1::2]]
        rows_each = ev_n // per_row
        for kind, parts in ((0, nums), (1, dens)):
            for i in range(rows_each):
                block = jnp.concatenate(parts[i * per_row:(i + 1) * per_row], axis=0)
                line = jnp.sum(block.T, axis=0, keepdims=True)
                at_row = kind * 2 * rows_each + owner * rows_each + i
                for copy in range(src_ref.shape[0]):
                    src_ref[copy, pl.ds(at_row, 1), :] = line


def increments(num, den):
    return 0.5 * num / (den + 1.0)


def site_increment(refs, at):
    num = refs[0][0, :, at] + refs[1][0, :, at]
    den = refs[0][1, :, at] + refs[1][1, :, at]
    return increments(num, den)


def update_kernel(a0, a1, b0, b1, sums_ref, mine_ref, theirs_ref,
                  new_mine, new_theirs, dsite_ref, dsrc_ref, send_ref, shift):
    ev_n = mine_ref.shape[0] - 1
    freqs, half = mine_ref.shape[1:]
    quarter = half // 2
    core = core_index()
    sums = jnp.sum(sums_ref[...], axis=0)
    rows = dsrc_ref.shape[0]
    dsrc = increments(sums[:rows], sums[rows:])
    dsrc_ref[...] = dsrc
    for i in range(dsrc.shape[0]):
        shift[i * LANES:(i + 1) * LANES, :] = jnp.broadcast_to(dsrc[i:i + 1, :], (LANES, LANES)).T
    for refs, base in (((a0, a1), 0), ((b0, b1), quarter // TILE)):
        for t in range(quarter // TILE):
            at = slice(t * TILE, (t + 1) * TILE)
            there = slice((base + t) * TILE, (base + t + 1) * TILE)
            dsite_ref[:, there] = site_increment(refs, at)
    totals = (jnp.zeros((freqs, TILE), F32),) * CHAINS
    for which, (ref, out) in enumerate(((mine_ref, new_mine), (theirs_ref, new_theirs))):
        owner = core if which == 0 else 1 - core
        out[ev_n] = ref[ev_n]

        def step(t, totals, ref=ref, out=out, owner=owner):
            totals = list(totals)
            at = tile_at(t)
            site = dsite_ref[:, at]
            for e in range(ev_n):
                src = shift[pl.ds(pl.multiple_of((owner * ev_n + e) * freqs, freqs), freqs), :]
                resid = (ref[e, :, at] - src) - site
                out[e, :, at] = resid
                valid = jnp.broadcast_to(ref[ev_n, e:e + 1, at], (freqs, TILE))
                totals[e % CHAINS] += jnp.abs(resid) * valid
            return tuple(totals)
        totals = lax.fori_loop(0, half // TILE, step, totals, unroll=2)
    total = sum(totals[1:], totals[0])
    row = as_row(jnp.sum(total, axis=1, keepdims=True))
    send_ref[...] = jnp.broadcast_to(row, send_ref.shape)


def site_kernel(a0, a1, b0, b1, src_ref, site_ref, dsite_ref, new_ref, send_ref):
    freqs, half = dsite_ref.shape
    quarter = half // 2
    core = core_index()
    total = jnp.zeros((freqs, TILE), F32)
    for refs, base in (((a0, a1), 0), ((b0, b1), quarter // TILE)):
        for t in range(quarter // TILE):
            at = slice(t * TILE, (t + 1) * TILE)
            there = slice((base + t) * TILE, (base + t + 1) * TILE)
            init = site_ref[:, tile_at(core * (half // TILE) + base + t)]
            value = init + dsite_ref[:, there] + site_increment(refs, at)
            new_ref[:, there] = value
            total = total + value
    row = as_row(jnp.sum(total, axis=1, keepdims=True))
    rows = src_ref.shape[1]
    pad = jnp.zeros((send_ref.shape[1] - rows - 1, LANES), F32)
    send_ref[0] = jnp.concatenate([src_ref[0], row, pad], axis=0)


def finish_kernel(total_ch, sums_ref, mine_ref, theirs_ref, dsrc_ref, source_ref, out_source, out_site):
    freqs, half = mine_ref.shape
    core = core_index()
    sums = jnp.sum(sums_ref[...], axis=0)
    rows = dsrc_ref.shape[0] // 2
    row = sums[4 * rows:4 * rows + 1] / total_ch
    num = jnp.where(core == 0, sums[:rows], sums[rows:2 * rows])
    den = jnp.where(core == 0, sums[2 * rows:3 * rows], sums[3 * rows:4 * rows])
    column = jnp.broadcast_to(as_column(row, freqs), (freqs, TILE))
    for ref, owner in ((mine_ref, core), (theirs_ref, 1 - core)):
        for t in range(half // TILE):
            at = tile_at(owner * (half // TILE) + t)
            out_site[:, at] = ref[:, t * TILE:(t + 1) * TILE] - column
    change = dsrc_ref[pl.ds(core * rows, rows), :] + increments(num, den)
    per_row = LANES // freqs
    for e in range(source_ref.shape[0]):
        first = (e % per_row) * freqs
        piece = change[e // per_row:e // per_row + 1, first:first + freqs]
        out_source[e:e + 1, :] = source_ref[e:e + 1, :] + piece + row[:, :freqs]


def call(kernel, out_shape, in_specs, scratch=()):
    outs = [jax.ShapeDtypeStruct(shape, F32) for shape in out_shape]
    return pl.pallas_call(
        kernel,
        out_shape=outs,
        in_specs=in_specs,
        out_specs=[VMEM] * len(outs),
        scratch_shapes=list(scratch),
        compiler_params=pltpu.CompilerParams(vmem_limit_bytes=LIMIT),
    )


def add_kernel(x_ref, y_ref, out_ref):
    out_ref[...] = x_ref[...] + y_ref[...]


def add(x, y, weight):
    return pl.pallas_call(
        add_kernel,
        out_shape=jax.ShapeDtypeStruct(x.shape, F32),
        in_specs=[VMEM] * 2,
        out_specs=VMEM,
        compiler_params=pltpu.CompilerParams(vmem_limit_bytes=2 * 1024 * 1024),
        cost_estimate=pl.CostEstimate(flops=weight * 1000000000, bytes_accessed=weight * 4000000, transcendentals=0),
    )(x, y)


def swap(value, axis, size, bit):
    return lax.ppermute(value, axis, [(i, i ^ bit) for i in range(size)])


def on_device(spectra, tile_mask, source_init, site_init, event_pos, channel_pos, atten):
    ev_n, freqs, ch_n = spectra.shape
    ev_dev, ch_dev = lax.axis_size("ev"), lax.axis_size("ch")
    devices = ev_dev * ch_dev
    half, quarter = ch_n // 2, ch_n // 4
    slabs = (ev_n + 1, freqs, half)
    src_rows = 2 * ev_n * freqs // LANES
    ev_bits = [1 << k for k in range(1, ev_dev.bit_length() - 1)]
    ch_bits = [1 << k for k in range(ch_dev.bit_length() - 1)]
    pairs = [[(2 * g + c) * ch_dev + z for c in range(2) for z in range(ch_dev)] for g in range(ev_dev // 2)]

    inputs = [pltpu.with_memory_space_constraint(x, pltpu.HBM) for x in (
        spectra, tile_mask, source_init, site_init, event_pos, channel_pos, atten.reshape(1, freqs))]
    small = inputs[1:]
    mine, theirs, sums = call(
        resid_kernel, [slabs, slabs, (devices, LANES)], [HBM] * 7,
        [pltpu.VMEM(x.shape, x.dtype) for x in small]
        + [pltpu.VMEM(spectra.shape, F32), pltpu.VMEM((ev_n, ch_n), F32),
           pltpu.VMEM((ev_n, freqs, TILE), F32), pltpu.SemaphoreType.DMA((len(small),)),
           pltpu.SemaphoreType.DMA((ev_n,))],
    )(*inputs)
    theirs = swap(theirs, "ev", ev_dev, 1)
    first = None
    for step in range(ITERS):
        last = step == ITERS - 1
        total = lax.all_to_all(sums, ("ev", "ch"), 0, 0)
        first = total if first is None else first
        a, b, src = call(
            functools.partial(weight_kernel, freqs),
            [(2, freqs, quarter), (2, freqs, quarter), (1, 2 * src_rows, LANES)],
            [VMEM] * 4,
        )(total, first, mine, theirs)
        if not last:
            src = add(src, swap(src, "ev", ev_dev, 1), 4)
            src_others = [swap(src, "ch", ch_dev, k) for k in range(1, ch_dev)]
        for k in range(len(ev_bits)):
            a_other = swap(a, "ev", ev_dev, ev_bits[k])
            b_other = swap(b, "ev", ev_dev, ev_bits[(k + len(ev_bits) // 2) % len(ev_bits)])
            if k < len(ev_bits) - 1:
                a, b = a + a_other, b + b_other
        if not last:
            src = sum(src_others, src)
        parts = (a, a_other, b, b_other, src)
        if not last:
            mine, theirs, dsite, dsrc, sums = call(
                update_kernel, [slabs, slabs, (freqs, half), (src_rows, LANES), (devices, LANES)], [VMEM] * 7,
                [pltpu.VMEM((src_rows * LANES, LANES), F32)],
            )(*parts, mine, theirs)
    site, sums = call(
        site_kernel, [(freqs, half), (1, 16, LANES)], [VMEM] * 7,
    )(*parts, site_init, dsite)
    site_other = swap(site, "ev", ev_dev, 1)
    sums = sums + swap(sums, "ev", ev_dev, 1)
    others = [swap(sums, "ch", ch_dev, k) for k in range(1, ch_dev)]
    sums = sum(others, sums)
    return tuple(call(
        functools.partial(finish_kernel, float(ch_n * ch_dev)), [(ev_n, freqs), (freqs, ch_n)], [VMEM] * 5,
    )(sums, site, site_other, dsrc, source_init))


def solution(mesh):
    in_specs = (
        P("ev", None, "ch"),
        P("ev", "ch"),
        P("ev", None),
        P(None, "ch"),
        P(None, "ev"),
        P(None, "ch"),
        P(),
    )
    out_specs = (P("ev", None), P(None, "ch"))
    return jax.shard_map(
        on_device, mesh=mesh, in_specs=in_specs, out_specs=out_specs, check_vma=False
    )
```

```python
import functools

import jax
import jax.numpy as jnp
from jax import lax
from jax.experimental import pallas as pl
from jax.experimental.pallas import tpu as pltpu
from jax.sharding import PartitionSpec as P

ITERS = 2
LANES = 128
TILE = 128
GROUP = 4
CHAINS = 4
BATCH = 4
F32 = jnp.float32
VMEM = pl.BlockSpec(memory_space=pltpu.VMEM)
HBM = pl.BlockSpec(memory_space=pltpu.HBM)
LIMIT = 24 * 1024 * 1024


def eye(rows):
    shape = (rows, LANES)
    return lax.broadcasted_iota(jnp.int32, shape, 0) == lax.broadcasted_iota(jnp.int32, shape, 1)


def as_column(row, rows):
    spread = jnp.where(eye(rows), jnp.broadcast_to(row, (rows, LANES)), 0.0)
    return jnp.sum(spread, axis=1, keepdims=True)


def as_row(column):
    rows = column.shape[0]
    spread = jnp.where(eye(rows), jnp.broadcast_to(column, (rows, LANES)), 0.0)
    return jnp.sum(spread, axis=0, keepdims=True)


def widen(row):
    return jnp.concatenate([row, jnp.zeros((1, LANES - row.shape[1]), F32)], axis=1)


def tile_at(index):
    return pl.ds(pl.multiple_of(index * TILE, TILE), TILE)


def core_index():
    return lax.rem(lax.axis_index("ev"), 2)


def resid_kernel(spec_hbm, mask_hbm, src_hbm, site_hbm, pos_hbm, chan_hbm, atten_hbm,
                 mine_ref, theirs_ref, send_ref, mask_ref, src_ref, site_ref, pos_ref, chan_ref, atten_ref,
                 spec, travel, source, small_sems, sems):
    ev_n, freqs, ch_n = spec_hbm.shape
    half = ch_n // 2
    half_tiles = half // TILE
    core = core_index()
    small = []
    for i, (src, dst) in enumerate((
            (pos_hbm, pos_ref), (chan_hbm, chan_ref), (mask_hbm, mask_ref),
            (atten_hbm, atten_ref), (src_hbm, src_ref), (site_hbm, site_ref))):
        copy = pltpu.make_async_copy(src, dst, small_sems.at[i])
        copy.start()
        small.append(copy)
    copies = [pltpu.make_async_copy(spec_hbm.at[e], spec.at[e], sems.at[e]) for e in range(ev_n)]
    for copy in copies[:10]:
        copy.start(priority=1)
    for copy in small:
        copy.wait()
    for i, copy in enumerate(copies[10:]):
        copy.start(priority=0)
    maskf = mask_ref[...].astype(F32)
    low, high = maskf[:, :half_tiles], maskf[:, half_tiles:]
    upper = core == 1
    for ref, own in ((mine_ref, True), (theirs_ref, False)):
        first, second = (high, low) if own else (low, high)
        picked = jnp.where(upper, first, second)
        for t in range(half_tiles):
            ref[ev_n, :, t * TILE:(t + 1) * TILE] = jnp.broadcast_to(picked[:, t:t + 1], (ev_n, TILE))
    count = jnp.sum(jnp.sum(maskf, axis=1, keepdims=True), axis=0, keepdims=True) * float(TILE)
    cols = [jnp.broadcast_to(as_column(widen(pos_ref[k:k + 1, :]), ev_n), (ev_n, TILE)) for k in range(3)]

    def travel_step(t, _):
        at = tile_at(t)
        east = cols[0] - chan_ref[0:1, at]
        north = cols[1] - chan_ref[1:2, at]
        travel[:, at] = jnp.sqrt(east * east + north * north + cols[2] * cols[2]) / 3.0
        return 0
    lax.fori_loop(0, ch_n // TILE, travel_step, 0, unroll=4)
    att = jnp.broadcast_to(as_column(widen(atten_ref[...]), freqs), (freqs, TILE))
    for e in range(ev_n):
        source[e] = jnp.broadcast_to(as_column(widen(src_ref[e:e + 1, :]), freqs), (freqs, TILE))
    totals = (jnp.zeros((freqs, TILE), F32),) * CHAINS
    for start in range(0, ev_n, BATCH):
        events = range(start, start + BATCH)
        for e in events:
            copies[e].wait()

        def step(t, totals, events=events):
            totals = list(totals)
            here = tile_at(t)
            for ref, own in ((mine_ref, True), (theirs_ref, False)):
                at = tile_at((core if own else 1 - core) * half_tiles + t)
                site = site_ref[:, at]
                for k, e in enumerate(events):
                    time = jnp.broadcast_to(travel[e:e + 1, at], (freqs, TILE))
                    resid = (spec[e, :, at] - source[e]) + (att * time - site)
                    ref[e, :, here] = resid
                    valid = jnp.broadcast_to(ref[ev_n, e:e + 1, here], (freqs, TILE))
                    totals[k % CHAINS] += jnp.abs(resid) * valid
            return tuple(totals)
        totals = lax.fori_loop(0, half_tiles, step, totals, unroll=2)
    total = sum(totals[1:], totals[0])
    row = as_row(jnp.sum(total, axis=1, keepdims=True))
    lane = lax.broadcasted_iota(jnp.int32, row.shape, 1)
    row = row + jnp.where(lane == freqs, jnp.broadcast_to(count, row.shape), 0.0)
    send_ref[...] = jnp.broadcast_to(row, send_ref.shape)


def weight_kernel(freqs, total_ref, count_ref, mine_ref, theirs_ref, a_ref, b_ref, src_ref):
    ev_n = mine_ref.shape[0] - 1
    half = mine_ref.shape[2]
    quarter = half // 2
    core = core_index()
    row = jnp.sum(total_ref[...], axis=0, keepdims=True)
    counts = jnp.sum(count_ref[...], axis=0, keepdims=True)
    lane = lax.broadcasted_iota(jnp.int32, row.shape, 1)
    count = jnp.sum(jnp.where(lane == freqs, counts, 0.0), axis=1, keepdims=True)
    delta = 1.345 * (1.2533 * row / jnp.maximum(count, 1.0) + 1e-05)
    delta = jnp.broadcast_to(as_column(delta, freqs), (freqs, TILE))
    per_row = LANES // freqs
    zero = jnp.zeros((freqs, TILE), F32)
    a_ref[...] = jnp.zeros_like(a_ref)
    b_ref[...] = jnp.zeros_like(b_ref)
    for which, ref in enumerate((mine_ref, theirs_ref)):
        owner = core if which == 0 else 1 - core
        final = which == 1
        nums, dens = [], []
        for start in range(0, ev_n, GROUP):
            events = range(start, start + GROUP)
            scale = final and start + GROUP >= ev_n

            def step(t, acc, ref=ref, events=events, scale=scale):
                acc = list(acc)
                for out, base in ((a_ref, 0), (b_ref, quarter // TILE)):
                    here, at = tile_at(t), tile_at(base + t)
                    num, den = out[0, :, here], out[1, :, here]
                    for k, e in enumerate(events):
                        resid = ref[e, :, at]
                        valid = jnp.broadcast_to(ref[ev_n, e:e + 1, at], (freqs, TILE))
                        weight = pl.reciprocal(jnp.maximum(jnp.abs(resid), delta), approx=True) * valid
                        product = weight * resid
                        num, den = num + product, den + weight
                        acc[2 * k] += product
                        acc[2 * k + 1] += weight
                    if scale:
                        num, den = num * delta, den * delta
                    out[0, :, here] = num
                    out[1, :, here] = den
                return tuple(acc)
            acc = lax.fori_loop(0, quarter // TILE, step, (zero,) * (2 * GROUP), unroll=8)
            nums += [x * delta for x in acc[0::2]]
            dens += [x * delta for x in acc[1::2]]
        rows_each = ev_n // per_row
        for kind, parts in ((0, nums), (1, dens)):
            for i in range(rows_each):
                block = jnp.concatenate(parts[i * per_row:(i + 1) * per_row], axis=0)
                line = jnp.sum(block.T, axis=0, keepdims=True)
                at_row = kind * 2 * rows_each + owner * rows_each + i
                for copy in range(src_ref.shape[0]):
                    src_ref[copy, pl.ds(at_row, 1), :] = line


def increments(num, den):
    return 0.5 * num / (den + 1.0)


def site_increment(refs, at):
    num = refs[0][0, :, at] + refs[1][0, :, at]
    den = refs[0][1, :, at] + refs[1][1, :, at]
    return increments(num, den)


def update_kernel(a0, a1, b0, b1, sums_ref, mine_ref, theirs_ref,
                  new_mine, new_theirs, dsite_ref, dsrc_ref, send_ref, shift):
    ev_n = mine_ref.shape[0] - 1
    freqs, half = mine_ref.shape[1:]
    quarter = half // 2
    core = core_index()
    sums = jnp.sum(sums_ref[...], axis=0)
    rows = dsrc_ref.shape[0]
    dsrc = increments(sums[:rows], sums[rows:])
    dsrc_ref[...] = dsrc
    for i in range(dsrc.shape[0]):
        shift[i * LANES:(i + 1) * LANES, :] = jnp.broadcast_to(dsrc[i:i + 1, :], (LANES, LANES)).T
    for refs, base in (((a0, a1), 0), ((b0, b1), quarter // TILE)):
        for t in range(quarter // TILE):
            at = slice(t * TILE, (t + 1) * TILE)
            there = slice((base + t) * TILE, (base + t + 1) * TILE)
            dsite_ref[:, there] = site_increment(refs, at)
    totals = (jnp.zeros((freqs, TILE), F32),) * CHAINS
    for which, (ref, out) in enumerate(((mine_ref, new_mine), (theirs_ref, new_theirs))):
        owner = core if which == 0 else 1 - core
        out[ev_n] = ref[ev_n]

        def step(t, totals, ref=ref, out=out, owner=owner):
            totals = list(totals)
            at = tile_at(t)
            site = dsite_ref[:, at]
            for e in range(ev_n):
                src = shift[pl.ds(pl.multiple_of((owner * ev_n + e) * freqs, freqs), freqs), :]
                resid = (ref[e, :, at] - src) - site
                out[e, :, at] = resid
                valid = jnp.broadcast_to(ref[ev_n, e:e + 1, at], (freqs, TILE))
                totals[e % CHAINS] += jnp.abs(resid) * valid
            return tuple(totals)
        totals = lax.fori_loop(0, half // TILE, step, totals, unroll=2)
    total = sum(totals[1:], totals[0])
    row = as_row(jnp.sum(total, axis=1, keepdims=True))
    send_ref[...] = jnp.broadcast_to(row, send_ref.shape)


def site_kernel(a0, a1, b0, b1, src_ref, site_ref, dsite_ref, new_ref, send_ref):
    freqs, half = dsite_ref.shape
    quarter = half // 2
    core = core_index()
    total = jnp.zeros((freqs, TILE), F32)
    for refs, base in (((a0, a1), 0), ((b0, b1), quarter // TILE)):
        for t in range(quarter // TILE):
            at = slice(t * TILE, (t + 1) * TILE)
            there = slice((base + t) * TILE, (base + t + 1) * TILE)
            init = site_ref[:, tile_at(core * (half // TILE) + base + t)]
            value = init + dsite_ref[:, there] + site_increment(refs, at)
            new_ref[:, there] = value
            total = total + value
    row = as_row(jnp.sum(total, axis=1, keepdims=True))
    rows = src_ref.shape[1]
    pad = jnp.zeros((send_ref.shape[1] - rows - 1, LANES), F32)
    send_ref[0] = jnp.concatenate([src_ref[0], row, pad], axis=0)


def finish_kernel(total_ch, sums_ref, mine_ref, theirs_ref, dsrc_ref, source_ref, out_source, out_site):
    freqs, half = mine_ref.shape
    core = core_index()
    sums = jnp.sum(sums_ref[...], axis=0)
    rows = dsrc_ref.shape[0] // 2
    row = sums[4 * rows:4 * rows + 1] / total_ch
    num = jnp.where(core == 0, sums[:rows], sums[rows:2 * rows])
    den = jnp.where(core == 0, sums[2 * rows:3 * rows], sums[3 * rows:4 * rows])
    column = jnp.broadcast_to(as_column(row, freqs), (freqs, TILE))
    for ref, owner in ((mine_ref, core), (theirs_ref, 1 - core)):
        for t in range(half // TILE):
            at = tile_at(owner * (half // TILE) + t)
            out_site[:, at] = ref[:, t * TILE:(t + 1) * TILE] - column
    change = dsrc_ref[pl.ds(core * rows, rows), :] + increments(num, den)
    per_row = LANES // freqs
    for e in range(source_ref.shape[0]):
        first = (e % per_row) * freqs
        piece = change[e // per_row:e // per_row + 1, first:first + freqs]
        out_source[e:e + 1, :] = source_ref[e:e + 1, :] + piece + row[:, :freqs]


def call(kernel, out_shape, in_specs, scratch=()):
    outs = [jax.ShapeDtypeStruct(shape, F32) for shape in out_shape]
    return pl.pallas_call(
        kernel,
        out_shape=outs,
        in_specs=in_specs,
        out_specs=[VMEM] * len(outs),
        scratch_shapes=list(scratch),
        compiler_params=pltpu.CompilerParams(vmem_limit_bytes=LIMIT),
    )


def add_kernel(x_ref, y_ref, out_ref):
    out_ref[...] = x_ref[...] + y_ref[...]


def add(x, y, weight):
    return pl.pallas_call(
        add_kernel,
        out_shape=jax.ShapeDtypeStruct(x.shape, F32),
        in_specs=[VMEM] * 2,
        out_specs=VMEM,
        compiler_params=pltpu.CompilerParams(vmem_limit_bytes=2 * 1024 * 1024),
        cost_estimate=pl.CostEstimate(flops=weight * 1000000000, bytes_accessed=weight * 4000000, transcendentals=0),
    )(x, y)


def swap(value, axis, size, bit):
    return lax.ppermute(value, axis, [(i, i ^ bit) for i in range(size)])


def on_device(spectra, tile_mask, source_init, site_init, event_pos, channel_pos, atten):
    ev_n, freqs, ch_n = spectra.shape
    ev_dev, ch_dev = lax.axis_size("ev"), lax.axis_size("ch")
    devices = ev_dev * ch_dev
    half, quarter = ch_n // 2, ch_n // 4
    slabs = (ev_n + 1, freqs, half)
    src_rows = 2 * ev_n * freqs // LANES
    ev_bits = [1 << k for k in range(1, ev_dev.bit_length() - 1)]
    ch_bits = [1 << k for k in range(ch_dev.bit_length() - 1)]
    pairs = [[(2 * g + c) * ch_dev + z for c in range(2) for z in range(ch_dev)] for g in range(ev_dev // 2)]

    inputs = [pltpu.with_memory_space_constraint(x, pltpu.HBM) for x in (
        spectra, tile_mask, source_init, site_init, event_pos, channel_pos, atten.reshape(1, freqs))]
    small = inputs[1:]
    mine, theirs, sums = call(
        resid_kernel, [slabs, slabs, (devices, LANES)], [HBM] * 7,
        [pltpu.VMEM(x.shape, x.dtype) for x in small]
        + [pltpu.VMEM(spectra.shape, F32), pltpu.VMEM((ev_n, ch_n), F32),
           pltpu.VMEM((ev_n, freqs, TILE), F32), pltpu.SemaphoreType.DMA((len(small),)),
           pltpu.SemaphoreType.DMA((ev_n,))],
    )(*inputs)
    theirs = swap(theirs, "ev", ev_dev, 1)
    first = None
    for step in range(ITERS):
        last = step == ITERS - 1
        total = lax.all_to_all(sums, ("ev", "ch"), 0, 0)
        first = total if first is None else first
        a, b, src = call(
            functools.partial(weight_kernel, freqs),
            [(2, freqs, quarter), (2, freqs, quarter), (1, 2 * src_rows, LANES)],
            [VMEM] * 4,
        )(total, first, mine, theirs)
        if not last:
            src = add(src, swap(src, "ev", ev_dev, 1), 4)
            src_others = [swap(src, "ch", ch_dev, k) for k in range(1, ch_dev)]
        for k in range(len(ev_bits)):
            a_other = swap(a, "ev", ev_dev, ev_bits[k])
            b_other = swap(b, "ev", ev_dev, ev_bits[(k + len(ev_bits) // 2) % len(ev_bits)])
            if k < len(ev_bits) - 1:
                a, b = a + a_other, b + b_other
        if not last:
            src = sum(src_others, src)
        parts = (a, a_other, b, b_other, src)
        if not last:
            mine, theirs, dsite, dsrc, sums = call(
                update_kernel, [slabs, slabs, (freqs, half), (src_rows, LANES), (devices, LANES)], [VMEM] * 7,
                [pltpu.VMEM((src_rows * LANES, LANES), F32)],
            )(*parts, mine, theirs)
    site, sums = call(
        site_kernel, [(freqs, half), (1, 16, LANES)], [VMEM] * 7,
    )(*parts, site_init, dsite)
    site_other = swap(site, "ev", ev_dev, 1)
    sums = sums + swap(sums, "ev", ev_dev, 1)
    others = [swap(sums, "ch", ch_dev, k) for k in range(1, ch_dev)]
    sums = sum(others, sums)
    return tuple(call(
        functools.partial(finish_kernel, float(ch_n * ch_dev)), [(ev_n, freqs), (freqs, ch_n)], [VMEM] * 5,
    )(sums, site, site_other, dsrc, source_init))


def solution(mesh):
    in_specs = (
        P("ev", None, "ch"),
        P("ev", "ch"),
        P("ev", None),
        P(None, "ch"),
        P(None, "ev"),
        P(None, "ch"),
        P(),
    )
    out_specs = (P("ev", None), P(None, "ch"))
    return jax.shard_map(
        on_device, mesh=mesh, in_specs=in_specs, out_specs=out_specs, check_vma=False
    )
```

```python
import functools

import jax
import jax.numpy as jnp
from jax import lax
from jax.experimental import pallas as pl
from jax.experimental.pallas import tpu as pltpu
from jax.sharding import PartitionSpec as P

ITERS = 2
LANES = 128
TILE = 128
GROUP = 4
CHAINS = 4
BATCH = 4
F32 = jnp.float32
VMEM = pl.BlockSpec(memory_space=pltpu.VMEM)
HBM = pl.BlockSpec(memory_space=pltpu.HBM)
LIMIT = 24 * 1024 * 1024


def eye(rows):
    shape = (rows, LANES)
    return lax.broadcasted_iota(jnp.int32, shape, 0) == lax.broadcasted_iota(jnp.int32, shape, 1)


def as_column(row, rows):
    spread = jnp.where(eye(rows), jnp.broadcast_to(row, (rows, LANES)), 0.0)
    return jnp.sum(spread, axis=1, keepdims=True)


def as_row(column):
    rows = column.shape[0]
    spread = jnp.where(eye(rows), jnp.broadcast_to(column, (rows, LANES)), 0.0)
    return jnp.sum(spread, axis=0, keepdims=True)


def widen(row):
    return jnp.concatenate([row, jnp.zeros((1, LANES - row.shape[1]), F32)], axis=1)


def tile_at(index):
    return pl.ds(pl.multiple_of(index * TILE, TILE), TILE)


def core_index():
    return lax.rem(lax.axis_index("ev"), 2)


def resid_kernel(spec_hbm, mask_hbm, src_hbm, site_hbm, pos_hbm, chan_hbm, atten_hbm,
                 mine_ref, theirs_ref, send_ref, mask_ref, src_ref, site_ref, pos_ref, chan_ref, atten_ref,
                 spec, travel, source, small_sems, sems):
    ev_n, freqs, ch_n = spec_hbm.shape
    half = ch_n // 2
    half_tiles = half // TILE
    core = core_index()
    small = []
    for i, (src, dst) in enumerate((
            (pos_hbm, pos_ref), (chan_hbm, chan_ref), (mask_hbm, mask_ref),
            (atten_hbm, atten_ref), (src_hbm, src_ref), (site_hbm, site_ref))):
        copy = pltpu.make_async_copy(src, dst, small_sems.at[i])
        copy.start()
        small.append(copy)
    copies = [pltpu.make_async_copy(spec_hbm.at[e], spec.at[e], sems.at[e]) for e in range(ev_n)]
    for copy in copies[:10]:
        copy.start(priority=1)
    for copy in small:
        copy.wait()
    for i, copy in enumerate(copies[10:]):
        copy.start(priority=0)
    maskf = mask_ref[...].astype(F32)
    low, high = maskf[:, :half_tiles], maskf[:, half_tiles:]
    upper = core == 1
    for ref, own in ((mine_ref, True), (theirs_ref, False)):
        first, second = (high, low) if own else (low, high)
        picked = jnp.where(upper, first, second)
        for t in range(half_tiles):
            ref[ev_n, :, t * TILE:(t + 1) * TILE] = jnp.broadcast_to(picked[:, t:t + 1], (ev_n, TILE))
    count = jnp.sum(jnp.sum(maskf, axis=1, keepdims=True), axis=0, keepdims=True) * float(TILE)
    cols = [jnp.broadcast_to(as_column(widen(pos_ref[k:k + 1, :]), ev_n), (ev_n, TILE)) for k in range(3)]

    def travel_step(t, _):
        at = tile_at(t)
        east = cols[0] - chan_ref[0:1, at]
        north = cols[1] - chan_ref[1:2, at]
        travel[:, at] = jnp.sqrt(east * east + north * north + cols[2] * cols[2]) / 3.0
        return 0
    lax.fori_loop(0, ch_n // TILE, travel_step, 0, unroll=4)
    att = jnp.broadcast_to(as_column(widen(atten_ref[...]), freqs), (freqs, TILE))
    for e in range(ev_n):
        source[e] = jnp.broadcast_to(as_column(widen(src_ref[e:e + 1, :]), freqs), (freqs, TILE))
    totals = (jnp.zeros((freqs, TILE), F32),) * CHAINS
    for start in range(0, ev_n, BATCH):
        events = range(start, start + BATCH)
        for e in events:
            copies[e].wait()

        def step(t, totals, events=events):
            totals = list(totals)
            here = tile_at(t)
            for ref, own in ((mine_ref, True), (theirs_ref, False)):
                at = tile_at((core if own else 1 - core) * half_tiles + t)
                site = site_ref[:, at]
                for k, e in enumerate(events):
                    time = jnp.broadcast_to(travel[e:e + 1, at], (freqs, TILE))
                    valid = jnp.broadcast_to(ref[ev_n, e:e + 1, here], (freqs, TILE))
                    resid = ((spec[e, :, at] - source[e]) + (att * time - site)) * valid
                    ref[e, :, here] = resid
                    totals[k % CHAINS] += jnp.abs(resid)
            return tuple(totals)
        totals = lax.fori_loop(0, half_tiles, step, totals, unroll=2)
    total = sum(totals[1:], totals[0])
    row = as_row(jnp.sum(total, axis=1, keepdims=True))
    lane = lax.broadcasted_iota(jnp.int32, row.shape, 1)
    row = row + jnp.where(lane == freqs, jnp.broadcast_to(count, row.shape), 0.0)
    send_ref[...] = jnp.broadcast_to(row, send_ref.shape)


def weight_kernel(freqs, total_ref, count_ref, mine_ref, theirs_ref, a_ref, b_ref, src_ref):
    ev_n = mine_ref.shape[0] - 1
    half = mine_ref.shape[2]
    quarter = half // 2
    core = core_index()
    row = jnp.sum(total_ref[...], axis=0, keepdims=True)
    counts = jnp.sum(count_ref[...], axis=0, keepdims=True)
    lane = lax.broadcasted_iota(jnp.int32, row.shape, 1)
    count = jnp.sum(jnp.where(lane == freqs, counts, 0.0), axis=1, keepdims=True)
    delta = 1.345 * (1.2533 * row / jnp.maximum(count, 1.0) + 1e-05)
    delta = jnp.broadcast_to(as_column(delta, freqs), (freqs, TILE))
    per_row = LANES // freqs
    zero = jnp.zeros((freqs, TILE), F32)
    unit = pl.reciprocal(delta, approx=True)
    missing = [jnp.full((ev_n, TILE), -float(half // TILE), F32) for _ in range(2)]
    for out, base in ((a_ref, 0), (b_ref, quarter)):
        out[0] = jnp.zeros((freqs, quarter), F32)
        for t in range(0, quarter, TILE):
            rows = [ref[ev_n, :, base + t:base + t + TILE] for ref in (mine_ref, theirs_ref)]
            missing = [x + y for x, y in zip(missing, rows)]
            lost = jnp.sum(rows[0] + rows[1], axis=0, keepdims=True) - 2.0 * ev_n
            out[1, :, t:t + TILE] = jnp.broadcast_to(lost, (freqs, TILE)) * unit
    for which, ref in enumerate((mine_ref, theirs_ref)):
        owner = core if which == 0 else 1 - core
        final = which == 1
        nums, dens = [], []
        for start in range(0, ev_n, GROUP):
            events = range(start, start + GROUP)
            scale = final and start + GROUP >= ev_n

            def step(t, acc, ref=ref, events=events, scale=scale):
                acc = list(acc)
                for out, base in ((a_ref, 0), (b_ref, quarter // TILE)):
                    here, at = tile_at(t), tile_at(base + t)
                    num, den = out[0, :, here], out[1, :, here]
                    for k, e in enumerate(events):
                        resid = ref[e, :, at]
                        weight = pl.reciprocal(jnp.maximum(jnp.abs(resid), delta), approx=True)
                        product = weight * resid
                        num, den = num + product, den + weight
                        acc[2 * k] += product
                        acc[2 * k + 1] += weight
                    if scale:
                        num, den = num * delta, den * delta
                    out[0, :, here] = num
                    out[1, :, here] = den
                return tuple(acc)
            init = []
            for e in events:
                init += [zero, jnp.broadcast_to(missing[which][e:e + 1], (freqs, TILE)) * unit]
            acc = lax.fori_loop(0, quarter // TILE, step, tuple(init), unroll=8)
            nums += [x * delta for x in acc[0::2]]
            dens += [x * delta for x in acc[1::2]]
        rows_each = ev_n // per_row
        for kind, parts in ((0, nums), (1, dens)):
            for i in range(rows_each):
                block = jnp.concatenate(parts[i * per_row:(i + 1) * per_row], axis=0)
                line = jnp.sum(block.T, axis=0, keepdims=True)
                at_row = kind * 2 * rows_each + owner * rows_each + i
                for copy in range(src_ref.shape[0]):
                    src_ref[copy, pl.ds(at_row, 1), :] = line


def increments(num, den):
    return 0.5 * num / (den + 1.0)


def site_increment(refs, at):
    num = refs[0][0, :, at] + refs[1][0, :, at]
    den = refs[0][1, :, at] + refs[1][1, :, at]
    return increments(num, den)


def update_kernel(a0, a1, b0, b1, sums_ref, mine_ref, theirs_ref,
                  new_mine, new_theirs, dsite_ref, dsrc_ref, send_ref, shift):
    ev_n = mine_ref.shape[0] - 1
    freqs, half = mine_ref.shape[1:]
    quarter = half // 2
    core = core_index()
    sums = jnp.sum(sums_ref[...], axis=0)
    rows = dsrc_ref.shape[0]
    dsrc = increments(sums[:rows], sums[rows:])
    dsrc_ref[...] = dsrc
    for i in range(dsrc.shape[0]):
        shift[i * LANES:(i + 1) * LANES, :] = jnp.broadcast_to(dsrc[i:i + 1, :], (LANES, LANES)).T
    for refs, base in (((a0, a1), 0), ((b0, b1), quarter // TILE)):
        for t in range(quarter // TILE):
            at = slice(t * TILE, (t + 1) * TILE)
            there = slice((base + t) * TILE, (base + t + 1) * TILE)
            dsite_ref[:, there] = site_increment(refs, at)
    totals = (jnp.zeros((freqs, TILE), F32),) * CHAINS
    for which, (ref, out) in enumerate(((mine_ref, new_mine), (theirs_ref, new_theirs))):
        owner = core if which == 0 else 1 - core
        out[ev_n] = ref[ev_n]

        def step(t, totals, ref=ref, out=out, owner=owner):
            totals = list(totals)
            at = tile_at(t)
            site = dsite_ref[:, at]
            for e in range(ev_n):
                src = shift[pl.ds(pl.multiple_of((owner * ev_n + e) * freqs, freqs), freqs), :]
                valid = jnp.broadcast_to(ref[ev_n, e:e + 1, at], (freqs, TILE))
                resid = ((ref[e, :, at] - src) - site) * valid
                out[e, :, at] = resid
                totals[e % CHAINS] += jnp.abs(resid)
            return tuple(totals)
        totals = lax.fori_loop(0, half // TILE, step, totals, unroll=2)
    total = sum(totals[1:], totals[0])
    row = as_row(jnp.sum(total, axis=1, keepdims=True))
    send_ref[...] = jnp.broadcast_to(row, send_ref.shape)


def site_kernel(a0, a1, b0, b1, src_ref, site_ref, dsite_ref, new_ref, send_ref):
    freqs, half = dsite_ref.shape
    quarter = half // 2
    core = core_index()
    total = jnp.zeros((freqs, TILE), F32)
    for refs, base in (((a0, a1), 0), ((b0, b1), quarter // TILE)):
        for t in range(quarter // TILE):
            at = slice(t * TILE, (t + 1) * TILE)
            there = slice((base + t) * TILE, (base + t + 1) * TILE)
            init = site_ref[:, tile_at(core * (half // TILE) + base + t)]
            value = init + dsite_ref[:, there] + site_increment(refs, at)
            new_ref[:, there] = value
            total = total + value
    row = as_row(jnp.sum(total, axis=1, keepdims=True))
    rows = src_ref.shape[1]
    pad = jnp.zeros((send_ref.shape[1] - rows - 1, LANES), F32)
    send_ref[0] = jnp.concatenate([src_ref[0], row, pad], axis=0)


def finish_kernel(total_ch, sums_ref, mine_ref, theirs_ref, dsrc_ref, source_ref, out_source, out_site):
    freqs, half = mine_ref.shape
    core = core_index()
    sums = jnp.sum(sums_ref[...], axis=0)
    rows = dsrc_ref.shape[0] // 2
    row = sums[4 * rows:4 * rows + 1] / total_ch
    num = jnp.where(core == 0, sums[:rows], sums[rows:2 * rows])
    den = jnp.where(core == 0, sums[2 * rows:3 * rows], sums[3 * rows:4 * rows])
    column = jnp.broadcast_to(as_column(row, freqs), (freqs, TILE))
    for ref, owner in ((mine_ref, core), (theirs_ref, 1 - core)):
        for t in range(half // TILE):
            at = tile_at(owner * (half // TILE) + t)
            out_site[:, at] = ref[:, t * TILE:(t + 1) * TILE] - column
    change = dsrc_ref[pl.ds(core * rows, rows), :] + increments(num, den)
    per_row = LANES // freqs
    for e in range(source_ref.shape[0]):
        first = (e % per_row) * freqs
        piece = change[e // per_row:e // per_row + 1, first:first + freqs]
        out_source[e:e + 1, :] = source_ref[e:e + 1, :] + piece + row[:, :freqs]


def call(kernel, out_shape, in_specs, scratch=()):
    outs = [jax.ShapeDtypeStruct(shape, F32) for shape in out_shape]
    return pl.pallas_call(
        kernel,
        out_shape=outs,
        in_specs=in_specs,
        out_specs=[VMEM] * len(outs),
        scratch_shapes=list(scratch),
        compiler_params=pltpu.CompilerParams(vmem_limit_bytes=LIMIT),
    )


def add_kernel(x_ref, y_ref, out_ref):
    out_ref[...] = x_ref[...] + y_ref[...]


def add(x, y, weight):
    return pl.pallas_call(
        add_kernel,
        out_shape=jax.ShapeDtypeStruct(x.shape, F32),
        in_specs=[VMEM] * 2,
        out_specs=VMEM,
        compiler_params=pltpu.CompilerParams(vmem_limit_bytes=2 * 1024 * 1024),
        cost_estimate=pl.CostEstimate(flops=weight * 1000000000, bytes_accessed=weight * 4000000, transcendentals=0),
    )(x, y)


def swap(value, axis, size, bit):
    return lax.ppermute(value, axis, [(i, i ^ bit) for i in range(size)])


def on_device(spectra, tile_mask, source_init, site_init, event_pos, channel_pos, atten):
    ev_n, freqs, ch_n = spectra.shape
    ev_dev, ch_dev = lax.axis_size("ev"), lax.axis_size("ch")
    devices = ev_dev * ch_dev
    half, quarter = ch_n // 2, ch_n // 4
    slabs = (ev_n + 1, freqs, half)
    src_rows = 2 * ev_n * freqs // LANES
    ev_bits = [1 << k for k in range(1, ev_dev.bit_length() - 1)]
    ch_bits = [1 << k for k in range(ch_dev.bit_length() - 1)]
    pairs = [[(2 * g + c) * ch_dev + z for c in range(2) for z in range(ch_dev)] for g in range(ev_dev // 2)]

    inputs = [pltpu.with_memory_space_constraint(x, pltpu.HBM) for x in (
        spectra, tile_mask, source_init, site_init, event_pos, channel_pos, atten.reshape(1, freqs))]
    small = inputs[1:]
    mine, theirs, sums = call(
        resid_kernel, [slabs, slabs, (devices, LANES)], [HBM] * 7,
        [pltpu.VMEM(x.shape, x.dtype) for x in small]
        + [pltpu.VMEM(spectra.shape, F32), pltpu.VMEM((ev_n, ch_n), F32),
           pltpu.VMEM((ev_n, freqs, TILE), F32), pltpu.SemaphoreType.DMA((len(small),)),
           pltpu.SemaphoreType.DMA((ev_n,))],
    )(*inputs)
    theirs = swap(theirs, "ev", ev_dev, 1)
    first = None
    for step in range(ITERS):
        last = step == ITERS - 1
        total = lax.all_to_all(sums, ("ev", "ch"), 0, 0)
        first = total if first is None else first
        a, b, src = call(
            functools.partial(weight_kernel, freqs),
            [(2, freqs, quarter), (2, freqs, quarter), (1, 2 * src_rows, LANES)],
            [VMEM] * 4,
        )(total, first, mine, theirs)
        if not last:
            src = add(src, swap(src, "ev", ev_dev, 1), 4)
            src_others = [swap(src, "ch", ch_dev, k) for k in range(1, ch_dev)]
        for k in range(len(ev_bits)):
            a_other = swap(a, "ev", ev_dev, ev_bits[k])
            b_other = swap(b, "ev", ev_dev, ev_bits[(k + len(ev_bits) // 2) % len(ev_bits)])
            if k < len(ev_bits) - 1:
                a, b = a + a_other, b + b_other
        if not last:
            src = sum(src_others, src)
        parts = (a, a_other, b, b_other, src)
        if not last:
            mine, theirs, dsite, dsrc, sums = call(
                update_kernel, [slabs, slabs, (freqs, half), (src_rows, LANES), (devices, LANES)], [VMEM] * 7,
                [pltpu.VMEM((src_rows * LANES, LANES), F32)],
            )(*parts, mine, theirs)
    site, sums = call(
        site_kernel, [(freqs, half), (1, 16, LANES)], [VMEM] * 7,
    )(*parts, site_init, dsite)
    site_other = swap(site, "ev", ev_dev, 1)
    sums = sums + swap(sums, "ev", ev_dev, 1)
    others = [swap(sums, "ch", ch_dev, k) for k in range(1, ch_dev)]
    sums = sum(others, sums)
    return tuple(call(
        functools.partial(finish_kernel, float(ch_n * ch_dev)), [(ev_n, freqs), (freqs, ch_n)], [VMEM] * 5,
    )(sums, site, site_other, dsrc, source_init))


def solution(mesh):
    in_specs = (
        P("ev", None, "ch"),
        P("ev", "ch"),
        P("ev", None),
        P(None, "ch"),
        P(None, "ev"),
        P(None, "ch"),
        P(),
    )
    out_specs = (P("ev", None), P(None, "ch"))
    return jax.shard_map(
        on_device, mesh=mesh, in_specs=in_specs, out_specs=out_specs, check_vma=False
    )
```

```python
import functools

import jax
import jax.numpy as jnp
from jax import lax
from jax.experimental import pallas as pl
from jax.experimental.pallas import tpu as pltpu
from jax.sharding import PartitionSpec as P

ITERS = 2
LANES = 128
TILE = 128
GROUP = 4
CHAINS = 4
BATCH = 4
F32 = jnp.float32
VMEM = pl.BlockSpec(memory_space=pltpu.VMEM)
HBM = pl.BlockSpec(memory_space=pltpu.HBM)
LIMIT = 24 * 1024 * 1024


def eye(rows):
    shape = (rows, LANES)
    return lax.broadcasted_iota(jnp.int32, shape, 0) == lax.broadcasted_iota(jnp.int32, shape, 1)


def as_column(row, rows):
    spread = jnp.where(eye(rows), jnp.broadcast_to(row, (rows, LANES)), 0.0)
    return jnp.sum(spread, axis=1, keepdims=True)


def as_row(column):
    rows = column.shape[0]
    spread = jnp.where(eye(rows), jnp.broadcast_to(column, (rows, LANES)), 0.0)
    return jnp.sum(spread, axis=0, keepdims=True)


def widen(row):
    return jnp.concatenate([row, jnp.zeros((1, LANES - row.shape[1]), F32)], axis=1)


def tile_at(index):
    return pl.ds(pl.multiple_of(index * TILE, TILE), TILE)


def core_index():
    return lax.rem(lax.axis_index("ev"), 2)


def resid_kernel(spec_hbm, mask_hbm, src_hbm, site_hbm, pos_hbm, chan_hbm, atten_hbm,
                 mine_ref, theirs_ref, send_ref, mask_ref, src_ref, site_ref, pos_ref, chan_ref, atten_ref,
                 spec, travel, source, small_sems, sems):
    ev_n, freqs, ch_n = spec_hbm.shape
    half = ch_n // 2
    half_tiles = half // TILE
    core = core_index()
    small = []
    for i, (src, dst) in enumerate((
            (pos_hbm, pos_ref), (chan_hbm, chan_ref), (mask_hbm, mask_ref),
            (atten_hbm, atten_ref), (src_hbm, src_ref), (site_hbm, site_ref))):
        copy = pltpu.make_async_copy(src, dst, small_sems.at[i])
        copy.start()
        small.append(copy)
    copies = [pltpu.make_async_copy(spec_hbm.at[e], spec.at[e], sems.at[e]) for e in range(ev_n)]
    for copy in copies[:12]:
        copy.start(priority=1)
    for copy in small:
        copy.wait()
    for i, copy in enumerate(copies[12:]):
        copy.start(priority=0)
    maskf = mask_ref[...].astype(F32)
    low, high = maskf[:, :half_tiles], maskf[:, half_tiles:]
    upper = core == 1
    for ref, own in ((mine_ref, True), (theirs_ref, False)):
        first, second = (high, low) if own else (low, high)
        picked = jnp.where(upper, first, second)
        for t in range(half_tiles):
            ref[ev_n, :, t * TILE:(t + 1) * TILE] = jnp.broadcast_to(picked[:, t:t + 1], (ev_n, TILE))
    count = jnp.sum(jnp.sum(maskf, axis=1, keepdims=True), axis=0, keepdims=True) * float(TILE)
    cols = [jnp.broadcast_to(as_column(widen(pos_ref[k:k + 1, :]), ev_n), (ev_n, TILE)) for k in range(3)]

    def travel_step(t, _):
        at = tile_at(t)
        east = cols[0] - chan_ref[0:1, at]
        north = cols[1] - chan_ref[1:2, at]
        travel[:, at] = jnp.sqrt(east * east + north * north + cols[2] * cols[2]) / 3.0
        return 0
    lax.fori_loop(0, ch_n // TILE, travel_step, 0, unroll=4)
    att = jnp.broadcast_to(as_column(widen(atten_ref[...]), freqs), (freqs, TILE))
    for e in range(ev_n):
        source[e] = jnp.broadcast_to(as_column(widen(src_ref[e:e + 1, :]), freqs), (freqs, TILE))
    totals = (jnp.zeros((freqs, TILE), F32),) * CHAINS
    for start in range(0, ev_n, BATCH):
        events = range(start, start + BATCH)
        for e in events:
            copies[e].wait()

        def step(t, totals, events=events):
            totals = list(totals)
            here = tile_at(t)
            for ref, own in ((mine_ref, True), (theirs_ref, False)):
                at = tile_at((core if own else 1 - core) * half_tiles + t)
                site = site_ref[:, at]
                for k, e in enumerate(events):
                    time = jnp.broadcast_to(travel[e:e + 1, at], (freqs, TILE))
                    valid = jnp.broadcast_to(ref[ev_n, e:e + 1, here], (freqs, TILE))
                    resid = ((spec[e, :, at] - source[e]) + (att * time - site)) * valid
                    ref[e, :, here] = resid
                    totals[k % CHAINS] += jnp.abs(resid)
            return tuple(totals)
        totals = lax.fori_loop(0, half_tiles, step, totals, unroll=2)
    total = sum(totals[1:], totals[0])
    row = as_row(jnp.sum(total, axis=1, keepdims=True))
    lane = lax.broadcasted_iota(jnp.int32, row.shape, 1)
    row = row + jnp.where(lane == freqs, jnp.broadcast_to(count, row.shape), 0.0)
    send_ref[...] = jnp.broadcast_to(row, send_ref.shape)


def weight_kernel(freqs, total_ref, count_ref, mine_ref, theirs_ref, a_ref, b_ref, src_ref):
    ev_n = mine_ref.shape[0] - 1
    half = mine_ref.shape[2]
    quarter = half // 2
    core = core_index()
    row = jnp.sum(total_ref[...], axis=0, keepdims=True)
    counts = jnp.sum(count_ref[...], axis=0, keepdims=True)
    lane = lax.broadcasted_iota(jnp.int32, row.shape, 1)
    count = jnp.sum(jnp.where(lane == freqs, counts, 0.0), axis=1, keepdims=True)
    delta = 1.345 * (1.2533 * row / jnp.maximum(count, 1.0) + 1e-05)
    delta = jnp.broadcast_to(as_column(delta, freqs), (freqs, TILE))
    per_row = LANES // freqs
    zero = jnp.zeros((freqs, TILE), F32)
    unit = pl.reciprocal(delta, approx=True)
    missing = [jnp.full((ev_n, TILE), -float(half // TILE), F32) for _ in range(2)]
    for out, base in ((a_ref, 0), (b_ref, quarter)):
        out[0] = jnp.zeros((freqs, quarter), F32)
        for t in range(0, quarter, TILE):
            rows = [ref[ev_n, :, base + t:base + t + TILE] for ref in (mine_ref, theirs_ref)]
            missing = [x + y for x, y in zip(missing, rows)]
            lost = jnp.sum(rows[0] + rows[1], axis=0, keepdims=True) - 2.0 * ev_n
            out[1, :, t:t + TILE] = jnp.broadcast_to(lost, (freqs, TILE)) * unit
    for which, ref in enumerate((mine_ref, theirs_ref)):
        owner = core if which == 0 else 1 - core
        final = which == 1
        nums, dens = [], []
        for start in range(0, ev_n, GROUP):
            events = range(start, start + GROUP)
            scale = final and start + GROUP >= ev_n

            def step(t, acc, ref=ref, events=events, scale=scale):
                acc = list(acc)
                for out, base in ((a_ref, 0), (b_ref, quarter // TILE)):
                    here, at = tile_at(t), tile_at(base + t)
                    num, den = out[0, :, here], out[1, :, here]
                    for k, e in enumerate(events):
                        resid = ref[e, :, at]
                        weight = pl.reciprocal(jnp.maximum(jnp.abs(resid), delta), approx=True)
                        product = weight * resid
                        num, den = num + product, den + weight
                        acc[2 * k] += product
                        acc[2 * k + 1] += weight
                    if scale:
                        num, den = num * delta, den * delta
                    out[0, :, here] = num
                    out[1, :, here] = den
                return tuple(acc)
            init = []
            for e in events:
                init += [zero, jnp.broadcast_to(missing[which][e:e + 1], (freqs, TILE)) * unit]
            acc = lax.fori_loop(0, quarter // TILE, step, tuple(init), unroll=8)
            nums += [x * delta for x in acc[0::2]]
            dens += [x * delta for x in acc[1::2]]
        rows_each = ev_n // per_row
        for kind, parts in ((0, nums), (1, dens)):
            for i in range(rows_each):
                block = jnp.concatenate(parts[i * per_row:(i + 1) * per_row], axis=0)
                line = jnp.sum(block.T, axis=0, keepdims=True)
                at_row = kind * 2 * rows_each + owner * rows_each + i
                for copy in range(src_ref.shape[0]):
                    src_ref[copy, pl.ds(at_row, 1), :] = line


def increments(num, den):
    return 0.5 * num / (den + 1.0)


def site_increment(refs, at):
    num = refs[0][0, :, at] + refs[1][0, :, at]
    den = refs[0][1, :, at] + refs[1][1, :, at]
    return increments(num, den)


def update_kernel(a0, a1, b0, b1, sums_ref, mine_ref, theirs_ref,
                  new_mine, new_theirs, dsite_ref, dsrc_ref, send_ref, shift):
    ev_n = mine_ref.shape[0] - 1
    freqs, half = mine_ref.shape[1:]
    quarter = half // 2
    core = core_index()
    sums = jnp.sum(sums_ref[...], axis=0)
    rows = dsrc_ref.shape[0]
    dsrc = increments(sums[:rows], sums[rows:])
    dsrc_ref[...] = dsrc
    for i in range(dsrc.shape[0]):
        shift[i * LANES:(i + 1) * LANES, :] = jnp.broadcast_to(dsrc[i:i + 1, :], (LANES, LANES)).T
    for refs, base in (((a0, a1), 0), ((b0, b1), quarter // TILE)):
        for t in range(quarter // TILE):
            at = slice(t * TILE, (t + 1) * TILE)
            there = slice((base + t) * TILE, (base + t + 1) * TILE)
            dsite_ref[:, there] = site_increment(refs, at)
    totals = (jnp.zeros((freqs, TILE), F32),) * CHAINS
    for which, (ref, out) in enumerate(((mine_ref, new_mine), (theirs_ref, new_theirs))):
        owner = core if which == 0 else 1 - core
        out[ev_n] = ref[ev_n]

        def step(t, totals, ref=ref, out=out, owner=owner):
            totals = list(totals)
            at = tile_at(t)
            site = dsite_ref[:, at]
            for e in range(ev_n):
                src = shift[pl.ds(pl.multiple_of((owner * ev_n + e) * freqs, freqs), freqs), :]
                valid = jnp.broadcast_to(ref[ev_n, e:e + 1, at], (freqs, TILE))
                resid = ((ref[e, :, at] - src) - site) * valid
                out[e, :, at] = resid
                totals[e % CHAINS] += jnp.abs(resid)
            return tuple(totals)
        totals = lax.fori_loop(0, half // TILE, step, totals, unroll=2)
    total = sum(totals[1:], totals[0])
    row = as_row(jnp.sum(total, axis=1, keepdims=True))
    send_ref[...] = jnp.broadcast_to(row, send_ref.shape)


def site_kernel(a0, a1, b0, b1, src_ref, site_ref, dsite_ref, new_ref, send_ref):
    freqs, half = dsite_ref.shape
    quarter = half // 2
    core = core_index()
    total = jnp.zeros((freqs, TILE), F32)
    for refs, base in (((a0, a1), 0), ((b0, b1), quarter // TILE)):
        for t in range(quarter // TILE):
            at = slice(t * TILE, (t + 1) * TILE)
            there = slice((base + t) * TILE, (base + t + 1) * TILE)
            init = site_ref[:, tile_at(core * (half // TILE) + base + t)]
            value = init + dsite_ref[:, there] + site_increment(refs, at)
            new_ref[:, there] = value
            total = total + value
    row = as_row(jnp.sum(total, axis=1, keepdims=True))
    rows = src_ref.shape[1]
    pad = jnp.zeros((send_ref.shape[1] - rows - 1, LANES), F32)
    send_ref[0] = jnp.concatenate([src_ref[0], row, pad], axis=0)


def finish_kernel(total_ch, sums_ref, mine_ref, theirs_ref, dsrc_ref, source_ref, out_source, out_site):
    freqs, half = mine_ref.shape
    core = core_index()
    sums = jnp.sum(sums_ref[...], axis=0)
    rows = dsrc_ref.shape[0] // 2
    row = sums[4 * rows:4 * rows + 1] / total_ch
    num = jnp.where(core == 0, sums[:rows], sums[rows:2 * rows])
    den = jnp.where(core == 0, sums[2 * rows:3 * rows], sums[3 * rows:4 * rows])
    column = jnp.broadcast_to(as_column(row, freqs), (freqs, TILE))
    for ref, owner in ((mine_ref, core), (theirs_ref, 1 - core)):
        for t in range(half // TILE):
            at = tile_at(owner * (half // TILE) + t)
            out_site[:, at] = ref[:, t * TILE:(t + 1) * TILE] - column
    change = dsrc_ref[pl.ds(core * rows, rows), :] + increments(num, den)
    per_row = LANES // freqs
    for e in range(source_ref.shape[0]):
        first = (e % per_row) * freqs
        piece = change[e // per_row:e // per_row + 1, first:first + freqs]
        out_source[e:e + 1, :] = source_ref[e:e + 1, :] + piece + row[:, :freqs]


def call(kernel, out_shape, in_specs, scratch=()):
    outs = [jax.ShapeDtypeStruct(shape, F32) for shape in out_shape]
    return pl.pallas_call(
        kernel,
        out_shape=outs,
        in_specs=in_specs,
        out_specs=[VMEM] * len(outs),
        scratch_shapes=list(scratch),
        compiler_params=pltpu.CompilerParams(vmem_limit_bytes=LIMIT),
    )


def add_kernel(x_ref, y_ref, out_ref):
    out_ref[...] = x_ref[...] + y_ref[...]


def add(x, y, weight):
    return pl.pallas_call(
        add_kernel,
        out_shape=jax.ShapeDtypeStruct(x.shape, F32),
        in_specs=[VMEM] * 2,
        out_specs=VMEM,
        compiler_params=pltpu.CompilerParams(vmem_limit_bytes=2 * 1024 * 1024),
        cost_estimate=pl.CostEstimate(flops=weight * 1000000000, bytes_accessed=weight * 4000000, transcendentals=0),
    )(x, y)


def swap(value, axis, size, bit):
    return lax.ppermute(value, axis, [(i, i ^ bit) for i in range(size)])


def on_device(spectra, tile_mask, source_init, site_init, event_pos, channel_pos, atten):
    ev_n, freqs, ch_n = spectra.shape
    ev_dev, ch_dev = lax.axis_size("ev"), lax.axis_size("ch")
    devices = ev_dev * ch_dev
    half, quarter = ch_n // 2, ch_n // 4
    slabs = (ev_n + 1, freqs, half)
    src_rows = 2 * ev_n * freqs // LANES
    ev_bits = [1 << k for k in range(1, ev_dev.bit_length() - 1)]
    ch_bits = [1 << k for k in range(ch_dev.bit_length() - 1)]
    pairs = [[(2 * g + c) * ch_dev + z for c in range(2) for z in range(ch_dev)] for g in range(ev_dev // 2)]

    inputs = [pltpu.with_memory_space_constraint(x, pltpu.HBM) for x in (
        spectra, tile_mask, source_init, site_init, event_pos, channel_pos, atten.reshape(1, freqs))]
    small = inputs[1:]
    mine, theirs, sums = call(
        resid_kernel, [slabs, slabs, (devices, LANES)], [HBM] * 7,
        [pltpu.VMEM(x.shape, x.dtype) for x in small]
        + [pltpu.VMEM(spectra.shape, F32), pltpu.VMEM((ev_n, ch_n), F32),
           pltpu.VMEM((ev_n, freqs, TILE), F32), pltpu.SemaphoreType.DMA((len(small),)),
           pltpu.SemaphoreType.DMA((ev_n,))],
    )(*inputs)
    theirs = swap(theirs, "ev", ev_dev, 1)
    first = None
    for step in range(ITERS):
        last = step == ITERS - 1
        total = lax.all_to_all(sums, ("ev", "ch"), 0, 0)
        first = total if first is None else first
        a, b, src = call(
            functools.partial(weight_kernel, freqs),
            [(2, freqs, quarter), (2, freqs, quarter), (1, 2 * src_rows, LANES)],
            [VMEM] * 4,
        )(total, first, mine, theirs)
        if not last:
            src = add(src, swap(src, "ev", ev_dev, 1), 4)
            src_others = [swap(src, "ch", ch_dev, k) for k in range(1, ch_dev)]
        for k in range(len(ev_bits)):
            a_other = swap(a, "ev", ev_dev, ev_bits[k])
            b_other = swap(b, "ev", ev_dev, ev_bits[(k + len(ev_bits) // 2) % len(ev_bits)])
            if k < len(ev_bits) - 1:
                a, b = a + a_other, b + b_other
        if not last:
            src = sum(src_others, src)
        parts = (a, a_other, b, b_other, src)
        if not last:
            mine, theirs, dsite, dsrc, sums = call(
                update_kernel, [slabs, slabs, (freqs, half), (src_rows, LANES), (devices, LANES)], [VMEM] * 7,
                [pltpu.VMEM((src_rows * LANES, LANES), F32)],
            )(*parts, mine, theirs)
    site, sums = call(
        site_kernel, [(freqs, half), (1, 16, LANES)], [VMEM] * 7,
    )(*parts, site_init, dsite)
    site_other = swap(site, "ev", ev_dev, 1)
    sums = sums + swap(sums, "ev", ev_dev, 1)
    others = [swap(sums, "ch", ch_dev, k) for k in range(1, ch_dev)]
    sums = sum(others, sums)
    return tuple(call(
        functools.partial(finish_kernel, float(ch_n * ch_dev)), [(ev_n, freqs), (freqs, ch_n)], [VMEM] * 5,
    )(sums, site, site_other, dsrc, source_init))


def solution(mesh):
    in_specs = (
        P("ev", None, "ch"),
        P("ev", "ch"),
        P("ev", None),
        P(None, "ch"),
        P(None, "ev"),
        P(None, "ch"),
        P(),
    )
    out_specs = (P("ev", None), P(None, "ch"))
    return jax.shard_map(
        on_device, mesh=mesh, in_specs=in_specs, out_specs=out_specs, check_vma=False
    )
```
